128 devices in a mesh: sec: 2 (over core), tx: 8 (over y, z_lo), ty: 8 (over z_hi, x).
Axes of the slice: x: 4, y: 4, z: 4 (z_hi: 2, z_lo: 2; z = z_hi * 2 + z_lo), core: 2. Of those that a mesh axis runs over, the one named last changes fastest.
Arguments:
- state: float32 [2, 72, 512, 2048], P('sec', None, 'tx', 'ty'), may hold values from -6 to 6
- coeffs: float32 [2, 3, 512, 2048], P('sec', None, 'tx', 'ty'), may hold values from 0.03 to 0.12
- forcing: float32 [4, 512, 2048], P(None, 'tx', 'ty'), may hold values from -4 to 3, as said below
- levels: int32 [512, 2048], P('tx', 'ty'), may hold values from 0 to 60, as said below
- remap: int32 [5, 2359296], P(None, ('tx', 'ty')), may hold values from 0 to 16383, as said below
Outputs:
- new_state: float32 [2, 72, 512, 2048], P('sec', None, 'tx', 'ty')
- surface_flux: float32 [2, 4, 512, 2048], P('sec', None, 'tx', 'ty')
The draws below stay inside these ranges and needn't reach their ends.
Inputs may be any that keep to these rules, and one draw needn't show every extreme that they name: `levels`: 0 marks land; 60 is reached. `remap`: each source tile's 36864 links go to nine tiles: tile row -1, 0 or + 4 and tile column -1, 0 or +1 from its own, cyclically; the links come in nine blocks of 4096, one per target tile in the order row step (-1, 0, +4) then column step (-1, 0, +1), and within a block in slot order 0 .. 4095; links of weight 0 carry nothing; weights are 0 to 4; every source tile fills all 4096 slots with nonzero weight toward at least one target tile. `forcing`: winds and precipitation within 3 in size; the previous sea surface temperature lies between -4 and -1.
All inputs are finite; a program needn't handle non-finite values.
Results may differ from the reference program's by a relative error of at most 0.000057.
Values sent between devices are 32-bit elements; how exact they have to be, the bound alone decides.
A program may use at most 128 MiB of HBM per device.

```python
import math
import jax
import jax.numpy as jnp

LEV = 72
OLEV = 60
CX = 64
CY = 256
CAP = 4096
ASTEPS = 3
OSTEPS = 2
TROWS = 8
TCOLS = 8
TILES = 64
CELLS = 16384
LINKS = 36864
NX = 512
NY = 2048


def draw_forcing(key, part):
    first, second = jax.random.split(key)
    winds = jax.random.truncated_normal(first, -3.0, 3.0, (3, NX, NY), jnp.float32)
    warmth = jax.random.uniform(second, (1, NX, NY), jnp.float32, -4.0, -2.0)
    return jnp.concatenate([winds, warmth], 0)


def draw_levels(key, part):
    first, second = jax.random.split(key)
    depth = jax.random.randint(first, (NX, NY), 1, OLEV + 1)
    land = jax.random.randint(second, (NX, NY), 0, 10) < 3
    depth = jnp.where(land, 0, depth)
    return depth.at[0, 0].set(OLEV).astype(jnp.int32)


def draw_remap(key, part):
    keys = jax.random.split(jax.random.fold_in(key, 7), 5)
    tile = jnp.arange(TILES, dtype=jnp.int32)
    tile_x = tile // TCOLS
    tile_y = tile % TCOLS
    near = jnp.arange(9, dtype=jnp.int32)
    row_steps = jnp.array([-1, 0, TROWS // 2], dtype=jnp.int32)
    off_x = row_steps[near // 3]
    off_y = near % 3 - 1
    target = (tile_x[:, None] + off_x[None, :]) % TROWS * TCOLS + (tile_y[:, None] + off_y[None, :]) % TCOLS
    counts = jax.random.randint(keys[0], (TILES, 9), 1, CAP + 1)
    full = jax.random.randint(keys[1], (TILES, 1), 0, 9)
    counts = jnp.where(near[None, :] == full, CAP, counts)
    slot = jnp.arange(CAP, dtype=jnp.int32)
    live = (slot[None, None, :] < counts[:, :, None]).astype(jnp.int32)
    source_row = jax.random.randint(keys[2], (TILES, 9, CAP), 0, CELLS)
    target_row = jax.random.randint(keys[3], (TILES, 9, CAP), 0, CELLS)
    weight = jax.random.randint(keys[4], (TILES, 9, CAP), 1, 5) * live
    target_tile = jnp.broadcast_to(target[:, :, None], (TILES, 9, CAP))
    slots = jnp.broadcast_to(slot[None, None, :], (TILES, 9, CAP))
    fields = jnp.stack([source_row, target_tile, slots, target_row, weight]).reshape(5, TILES, LINKS)
    return fields.reshape(5, TILES * LINKS).astype(jnp.int32)


def steps_of(own_key, dims, pieces, smallest, top_value):
    loudness, own = 1.0, jax.random.fold_in(own_key, 6)
    for axis_at, shards_of in pieces:
        heights = jnp.exp(jax.random.uniform(jax.random.fold_in(own, axis_at), (shards_of,), jnp.float32, smallest / len(pieces), top_value / len(pieces)))
        loudness = loudness * jnp.repeat(heights, dims[axis_at] // shards_of).reshape([-1 if axis == axis_at else 1 for axis in range(len(dims))])
    return loudness


def scatter_about(stream_key, dims, deviation, bound, cuts=(), kind=jnp.bfloat16):
    drawn = jax.random.normal(stream_key, dims, jnp.float32) * deviation
    if len(cuts) > 0:
        drawn = steps_of(stream_key, dims, cuts, -0.22, 0.18) * drawn
    return jnp.clip(drawn, min=-bound, max=bound).astype(kind)


def setup_inputs(seed: int = 0) -> dict:
    key_list = jax.random.split(jax.random.key(seed), 6)
    state = scatter_about(key_list[0], (2, LEV, NX, NY), 1.0, 6.0, ((0, 2), (2, 8), (3, 8)), jnp.float32)
    coeffs = jnp.clip(jnp.exp(math.log(0.12) - 1.3862944 * jax.random.uniform(key_list[1], (2, 3, NX, NY), jnp.float32) ** steps_of(key_list[1], (2, 3, NX, NY), ((0, 2), (2, 8), (3, 8)), -0.2, 0.2)), 0.03, 0.12)
    forcing = draw_forcing(jax.random.fold_in(key_list[5], 71), 0)
    levels = draw_levels(jax.random.fold_in(key_list[5], 71), 0)
    remap = draw_remap(jax.random.fold_in(key_list[5], 71), 0)
    return dict(state=state, coeffs=coeffs, forcing=forcing, levels=levels, remap=remap)


def advance(field, depth, kappa, mixing, stress):
    level_index = jnp.arange(field.shape[0], dtype=jnp.float32)[:, None, None]
    wet = (level_index < depth).astype(jnp.float32)
    horiz = jnp.zeros_like(field)
    nears = []
    for axis, offset in ((1, -1), (1, 1), (2, -1), (2, 1)):
        near = jnp.roll(field, offset, axis)
        near_kap = jnp.roll(kappa, offset, axis - 1)
        near_dep = jnp.roll(depth, offset, axis - 1)
        near_wet = (level_index < near_dep).astype(jnp.float32)
        horiz = horiz + 0.5 * (kappa + near_kap) * wet * near_wet * (near - field)
        nears.append(near)
    zero = jnp.zeros((1,) + field.shape[1:], jnp.float32)
    above = jnp.concatenate([field[1:], zero], 0)
    above_wet = jnp.concatenate([wet[1:], zero], 0)
    below = jnp.concatenate([zero, field[:-1]], 0)
    below_wet = jnp.concatenate([zero, wet[:-1]], 0)
    vert = mixing * (above_wet * (above - field) + below_wet * (below - field))
    if stress is None:
        return field + wet * (horiz + vert)
    decay = jnp.exp(-level_index / 8.0)
    advect = 0.5 * decay * (stress[0] * (nears[0] - nears[1]) + stress[1] * (nears[2] - nears[3]))
    return field + wet * (horiz + vert - advect)

def remap_fluxes(flux, remap):
    tiles = TROWS * TCOLS
    per_tile = flux.reshape(4, TROWS, CX, TCOLS, CY).transpose(1, 3, 2, 4, 0).reshape(tiles, CX * CY, 4)
    links = remap.reshape(5, tiles, LINKS)
    owner = jnp.arange(tiles, dtype=jnp.int32)[:, None]
    weight = links[4].astype(jnp.float32)
    picked = per_tile[owner, links[0]] * weight[:, :, None]
    data = jnp.concatenate([picked, weight[:, :, None]], 2).reshape(-1, 5)
    target = (links[1] * (CX * CY) + links[3]).reshape(-1)
    sums = jax.ops.segment_sum(data, target, num_segments=tiles * CX * CY)
    return sums.reshape(TROWS, TCOLS, CX, CY, 5).transpose(4, 0, 2, 1, 3).reshape(5, NX, NY)

def reference(state, coeffs, forcing, levels, remap):
    atm = state[0]
    full_depth = jnp.full((NX, NY), LEV, jnp.float32)
    for step in range(ASTEPS):
        heat = coeffs[0, 2] * (atm[0] - forcing[3])
        atm = advance(atm, full_depth, coeffs[0, 0], coeffs[0, 1], None)
        atm = atm.at[0].add(-heat)
    heat = coeffs[0, 2] * (atm[0] - forcing[3])
    speed = jnp.sqrt(1.0 + forcing[0] * forcing[0] + forcing[1] * forcing[1])
    atm_flux = jnp.stack([heat, forcing[2] - 0.5 * heat, 0.2 * speed * forcing[0], 0.2 * speed * forcing[1]])
    sums = remap_fluxes(atm_flux, remap)
    remapped = sums[:4] / jnp.maximum(sums[4], 1.0)
    surface = (levels > 0).astype(jnp.float32)
    fix = (jnp.sum(heat) - jnp.sum(surface * remapped[0])) / jnp.maximum(jnp.sum(surface), 1.0)
    ocean_flux = surface * jnp.stack([remapped[0] + fix, remapped[1], remapped[2], remapped[3]])
    ocean = state[1]
    depth = levels.astype(jnp.float32)
    for step in range(OSTEPS):
        ocean = advance(ocean, depth, coeffs[1, 0], coeffs[1, 1], (ocean_flux[2], ocean_flux[3]))
        ocean = ocean.at[0].add(surface * 4.0 * coeffs[1, 2] * (ocean_flux[0] + 0.3 * ocean_flux[1]))
    return (jnp.stack([atm, ocean]), jnp.stack([atm_flux, ocean_flux]))
```

```python
import math

import jax
import jax.numpy as jnp
from jax import lax
from jax.experimental import pallas as pl
from jax.experimental.pallas import tpu as pltpu
from jax.sharding import PartitionSpec as P

LEV, OLEV, CX, CY = 72, 60, 64, 256
CAP = 4096
TAB = 8
CH = 24
NCH = LEV // CH
F32, BF16 = jnp.float32, jnp.bfloat16
MESH = pl.DeviceIdType.MESH


def hi_lo(x):
    high = x.astype(BF16)
    return high, (x - high.astype(F32)).astype(BF16)


def wide(x, count):
    return jnp.concatenate([x] * count, 1)


def kernel(
    state, coef, forc, lev, remap, out_state, out_flux,
    buf, rsend, csend, rrecv, crecv, cf, lnk_s, lnk_r, val_s, val_r, acc, fb, iota, dec,
    rem, hst, qb, qrow, qcol, red, red1, red2,
    in_sem, out_sem, hs_sem, hr_sem, ls_sem, lr_sem, vs_sem, vr_sem, rs_sem, rr_sem,
    qs_sem, qr_sem, p1s_sem, p1r_sem, p2s_sem, p2r_sem,
):
    sec, tx, ty = lax.axis_index("sec"), lax.axis_index("tx"), lax.axis_index("ty")
    is_atm = sec == 0
    is_ocn = sec == 1

    def near(dx, dy):
        return (sec, lax.rem(tx + dx + 8, 8), lax.rem(ty + dy + 8, 8))

    barrier = pltpu.get_barrier_semaphore()
    for dx in (-1, 0, 1, 4):
        for dy in (-1, 0, 1):
            if dx != 0 or dy != 0:
                pl.semaphore_signal(barrier, 1, device_id=near(dx, dy), device_id_type=MESH)
    for dy in range(2, 7):
        pl.semaphore_signal(barrier, 1, device_id=near(0, dy), device_id_type=MESH)
    for dx in range(8):
        pl.semaphore_signal(
            barrier, 1, device_id=(1 - sec, lax.rem(tx + dx, 8), ty), device_id_type=MESH
        )

    def state_in(ch):
        return pltpu.make_async_copy(
            state.at[0, pl.ds(ch * CH, CH)],
            buf.at[0, pl.ds(ch * CH, CH), pl.ds(TAB, CX)],
            in_sem.at[ch],
        )

    for ch in range(NCH):
        state_in(ch).start()

    for n in range(9):
        lnk_s[n] = remap[3:5, n * CAP : (n + 1) * CAP]
    iota[...] = lax.broadcasted_iota(jnp.int32, (CY, 128), 0).astype(F32).astype(BF16)
    dec[...] = 0.5 * jnp.exp(lax.broadcasted_iota(jnp.int32, (LEV, 128), 0).astype(F32) * (-1 / 8))
    lane = lax.broadcasted_iota(jnp.int32, (8, 128), 1)

    kap, mix, c2 = coef[0, 0], coef[0, 1], coef[0, 2]
    depth = jnp.where(is_atm, jnp.full((CX, CY), float(LEV), F32), lev[...].astype(F32))
    surface = (lev[...] > 0).astype(F32)

    pl.semaphore_wait(barrier, 24)

    def target_of(n):
        row_step = n // 3
        return near(row_step - 1 + 3 * (row_step // 2), n % 3 - 1)

    def lnk_copy(n):
        return pltpu.make_async_remote_copy(
            lnk_s.at[n], lnk_r.at[n], ls_sem.at[n], lr_sem.at[n],
            device_id=target_of(n), device_id_type=MESH,
        )

    def val_copy(n):
        return pltpu.make_async_remote_copy(
            val_s.at[n], val_r.at[n], vs_sem.at[n], vr_sem.at[n],
            device_id=target_of(n), device_id_type=MESH,
        )

    def halo_copies(s, ch):
        out = []
        for d, (there, low) in enumerate(
            ((near(1, 0), 0), (near(-1, 0), 1), (near(0, 1), 0), (near(0, -1), 1))
        ):
            send, recv = (rsend, rrecv) if d < 2 else (csend, crecv)
            out.append(
                pltpu.make_async_remote_copy(
                    send.at[s, ch, low], recv.at[s, ch, low],
                    hs_sem.at[s, ch, d], hr_sem.at[s, ch, d],
                    device_id=there, device_id_type=MESH,
                )
            )
        return out

    def pack_low(value, k):
        return pltpu.roll(value[:, :128], k, 1)

    def pack_high(value, k):
        return pltpu.roll(value[:, 128:], k + 1, 1)

    rsend[0, 0, 0, CH : CH + 8] = jnp.zeros((8, CY), F32)
    rsend[0, 0, 1, CH : CH + 8] = jnp.zeros((8, CY), F32)
    for at, plane in enumerate((kap, depth, c2)):
        rsend[0, 0, 0, CH + at : CH + at + 1] = plane[CX - 1 : CX]
        rsend[0, 0, 1, CH + at : CH + at + 1] = plane[0:1]
    for ch in range(NCH):
        state_in(ch).wait()

        def row_edges(kk, carry, ch=ch):
            k = ch * CH + kk
            rsend[0, ch, 0, pl.ds(kk, 1)] = buf[0, k, TAB + CX - 1 : TAB + CX]
            rsend[0, ch, 1, pl.ds(kk, 1)] = buf[0, k, TAB : TAB + 1]
            return carry

        lax.fori_loop(0, CH, row_edges, 0, unroll=8)
        for g in range(8):
            rows = slice(TAB + 8 * g, TAB + 8 * g + 8)

            def col_edges(kk, packs, ch=ch, rows=rows):
                value = buf[0, ch * CH + kk, rows]
                here = lane == kk
                return (
                    jnp.where(here, pack_high(value, kk), packs[0]),
                    jnp.where(here, pack_low(value, kk), packs[1]),
                )

            zero = jnp.zeros((8, 128), F32)
            packs = lax.fori_loop(0, CH, col_edges, (zero, zero), unroll=4)
            if ch == 0:
                for at, plane in enumerate((kap, depth, c2)):
                    part = plane[8 * g : 8 * g + 8]
                    packs = (
                        jnp.where(lane == CH + at, pack_high(part, CH + at), packs[0]),
                        jnp.where(lane == CH + at, pack_low(part, CH + at), packs[1]),
                    )
            csend[0, ch, 0, 8 * g : 8 * g + 8] = packs[0]
            csend[0, ch, 1, 8 * g : 8 * g + 8] = packs[1]
        for copy in halo_copies(0, ch):
            copy.start()

    for n in range(9):
        if n != 4:
            lnk_copy(n).start()

    lane_all = lax.broadcasted_iota(jnp.int32, (CX, CY), 1)

    def shifted(plane, at):
        low_row = rrecv[0, 0, 0, CH + at : CH + at + 1]
        high_row = rrecv[0, 0, 1, CH + at : CH + at + 1]
        low_col = crecv[0, 0, 0][:, CH + at : CH + at + 1]
        high_col = crecv[0, 0, 1][:, CH + at : CH + at + 1]
        return (
            jnp.concatenate([low_row, plane[:-1]], 0),
            jnp.concatenate([plane[1:], high_row], 0),
            jnp.where(lane_all == 0, low_col, pltpu.roll(plane, 1, 1)),
            jnp.where(lane_all == CY - 1, high_col, pltpu.roll(plane, CY - 1, 1)),
        )

    def static_part():
        total = jnp.zeros((CX, CY), F32)
        for at, other in enumerate(shifted(kap, 0)):
            half = 0.5 * (kap + other)
            cf[at] = half
            total = total + half
        cf[4] = mix
        cf[5] = (1.0 - total) - 2.0 * mix

    def halos_arrived(s, ch):
        for copy in halo_copies(s, ch):
            copy.wait_recv()

        @pl.when(jnp.logical_and(s == 0, ch == 0))
        def _():
            static_part()
            for at, other in enumerate(shifted(depth, 1)):
                cf[6 + at] = other

    def rows_in(s, slot, ch, count):
        def one(kk, carry):
            k = ch * CH + kk
            buf[slot, k, TAB - 1 : TAB] = rrecv[s, ch, 0, pl.ds(kk, 1)]
            buf[slot, k, TAB + CX : TAB + CX + 1] = rrecv[s, ch, 1, pl.ds(kk, 1)]
            return carry

        lax.fori_loop(0, count, one, 0, unroll=4)

    lane_wide = lax.broadcasted_iota(jnp.int32, (8, CY), 1)

    def sides(slot, k, kk, g, value, col_low, col_high):
        at = TAB + 8 * g
        up = buf[slot, k, at - 1 : at + 7]
        down = buf[slot, k, at + 1 : at + 9]
        back = lax.rem(128 - kk, 128)
        low = pltpu.roll(col_low, back, 1)
        high = pltpu.roll(col_high, lax.rem(127 - kk + 128, 128), 1)
        left = jnp.where(lane_wide == 0, wide(low, 2), pltpu.roll(value, 1, 1))
        right = jnp.where(lane_wide == CY - 1, wide(high, 2), pltpu.roll(value, CY - 1, 1))
        return up, down, left, right

    @pl.when(is_atm)
    def _():
        def piece(t, carry):
            s, ch = t // NCH, t % NCH
            slot = s % 2
            halos_arrived(s, ch)
            rows_in(s, slot, ch, CH)
            first = ch * CH
            after = s + 1
            for g in range(8):
                part = slice(8 * g, 8 * g + 8)
                rows = slice(TAB + 8 * g, TAB + 8 * g + 8)
                c_up, c_down, c_left, c_right, c_mix, c_own = [cf[i, part] for i in range(6)]
                col_low, col_high = crecv[s, ch, 0, part], crecv[s, ch, 1, part]
                top = buf[slot, 0, rows]
                heat = coef[0, 2, part] * (top - forc[3, part])
                extra = jnp.where(ch == 0, -heat, 0.0)

                def level(kk, held):
                    before, value, extra, pack0, pack1 = held
                    k = first + kk
                    following = buf[slot, jnp.minimum(k + 1, LEV - 1), rows]
                    up, down, left, right = sides(slot, k, kk, g, value, col_low, col_high)
                    new = (c_own * value + extra) + c_mix * (before + following)
                    new = new + (c_up * up + c_down * down) + (c_left * left + c_right * right)
                    buf[1 - slot, k, rows] = new
                    here = lane == kk
                    pack0 = jnp.where(here, pack_high(new, kk), pack0)
                    pack1 = jnp.where(here, pack_low(new, kk), pack1)
                    if g == 7:
                        rsend[after, ch, 0, pl.ds(kk, 1)] = new[7:8]
                    if g == 0:
                        rsend[after, ch, 1, pl.ds(kk, 1)] = new[0:1]
                    return value, following, jnp.zeros_like(extra), pack0, pack1

                zero = jnp.zeros((8, 128), F32)
                held = (buf[slot, jnp.maximum(first - 1, 0), rows], buf[slot, first, rows], extra, zero, zero)
                held = lax.fori_loop(0, CH, level, held, unroll=4)
                csend[after, ch, 0, part] = held[3]
                csend[after, ch, 1, part] = held[4]

            @pl.when(s < 2)
            def _():
                for copy in halo_copies(after, ch):
                    copy.start()

            return carry

        lax.fori_loop(0, 3 * NCH, piece, 0)
        pltpu.make_async_copy(buf.at[1, :, pl.ds(TAB, CX)], out_state.at[0], out_sem).start()
        heat = c2 * (buf[1, 0, TAB : TAB + CX] - forc[3])
        out_flux[0, 0] = heat
        out_flux[0, 1] = forc[2] - 0.5 * heat

    speed = 0.2 * jnp.sqrt(1.0 + forc[0] * forc[0] + forc[1] * forc[1])

    @pl.when(is_atm)
    def _():
        out_flux[0, 2] = speed * forc[0]
        out_flux[0, 3] = speed * forc[1]

    @pl.when(is_ocn)
    def _():
        out_flux[0, 0] = speed * forc[0]
        out_flux[0, 1] = speed * forc[1]

    for c in range(2):
        high, low = hi_lo(out_flux[0, c])
        fb[CX * c : CX * (c + 1)] = high
        fb[2 * CX + CX * c : 2 * CX + CX * (c + 1)] = low
    one, none = jnp.array(1, BF16), jnp.array(0, BF16)

    def pick(t, carry):
        n = lax.rem(t + 5, 9)
        at = pl.multiple_of(n * CAP, CAP)
        source = remap[0:1, pl.ds(at, CAP)]
        weight = remap[4:5, pl.ds(at, CAP)].astype(F32)
        col = (source & (CY - 1)).astype(F32).astype(BF16)
        hot = jnp.where(wide(iota[...], CAP // 128) == col, one, none)
        product = jnp.dot(fb[...], hot, preferred_element_type=F32)
        here = lax.broadcasted_iota(jnp.int32, (CX, CAP), 0) == (source >> 8)
        for c in range(2):
            both = product[CX * c : CX * (c + 1)] + product[2 * CX + CX * c : 2 * CX + CX * (c + 1)]
            val_s[n, c : c + 1] = jnp.sum(jnp.where(here, both, 0.0), 0, keepdims=True) * weight

        @pl.when(n != 4)
        def _():
            val_copy(n).start()

        return carry

    lax.fori_loop(0, 9, pick, 0)
    lnk_r[4] = lnk_s[4]
    val_r[4] = val_s[4]
    acc[...] = jnp.zeros_like(acc)

    def add(t, carry):
        n = lax.rem(t + 4, 9)

        @pl.when(n != 4)
        def _():
            lnk_copy(n).wait_recv()
            val_copy(n).wait_recv()

        target = lnk_r[n, 0:1]
        weight = lnk_r[n, 1:2].astype(F32).astype(BF16)
        col = (target & (CY - 1)).astype(F32).astype(BF16)
        row = (target >> 8).astype(F32).astype(BF16)
        index = wide(iota[...], CAP // 128)
        hot = jnp.where(index == col, one, none)
        here = index[:CX] == row
        high0, low0 = hi_lo(val_r[n, 0:1])
        high1, low1 = hi_lo(val_r[n, 1:2])
        spread = jnp.concatenate(
            [jnp.where(here, x, none) for x in (high0, high1, low0, low1, weight)], 0
        )
        acc[...] += lax.dot_general(
            spread, hot, (((1,), (1,)), ((), ())), preferred_element_type=F32
        )
        return carry

    lax.fori_loop(0, 9, add, 0)
    per = 1.0 / jnp.maximum(acc[4 * CX : 5 * CX], 1.0)
    rem[0] = (acc[0:CX] + acc[2 * CX : 3 * CX]) * per
    rem[1] = (acc[CX : 2 * CX] + acc[3 * CX : 4 * CX]) * per

    hand_over = pltpu.make_async_remote_copy(
        rem, hst, rs_sem, rr_sem, device_id=(1 - sec, tx, ty), device_id_type=MESH
    )

    def along_ty(d):
        return pltpu.make_async_remote_copy(
            red, red1.at[d], p1s_sem.at[d], p1r_sem.at[d],
            device_id=near(0, d), device_id_type=MESH,
        )

    def along_tx(d):
        return pltpu.make_async_remote_copy(
            red1.at[0], red2.at[d], p2s_sem.at[d], p2r_sem.at[d],
            device_id=(1 - sec, lax.rem(tx + d, 8), ty), device_id_type=MESH,
        )

    def folded(plane):
        total = plane[0:8]
        for g in range(1, 8):
            total = total + plane[8 * g : 8 * g + 8]
        return total[:, :128] + total[:, 128:]

    @pl.when(is_atm)
    def _():
        hand_over.start()
        red[0:8] = folded(out_flux[0, 0] - surface * rem[0])
        red[8:16] = folded(surface)
        for d in range(1, 8):
            along_ty(d).start()
        total = red[...]
        for d in range(1, 8):
            along_ty(d).wait_recv()
            total = total + red1[d]
        red1[0] = total
        for d in range(8):
            along_tx(d).start()
        for d in range(1, 8):
            along_ty(d).wait_send()
        for d in range(8):
            along_tx(d).wait_send()
        hand_over.wait_send()
        pltpu.make_async_copy(buf.at[1, :, pl.ds(TAB, CX)], out_state.at[0], out_sem).wait()

    @pl.when(is_ocn)
    def _():
        stress = (surface * rem[0], surface * rem[1])
        out_flux[0, 2] = stress[0]
        out_flux[0, 3] = stress[1]

        def levels(s, ch, start, stop, packed):
            slot = s
            first = ch * CH
            for g in range(8):
                part = slice(8 * g, 8 * g + 8)
                rows = slice(TAB + 8 * g, TAB + 8 * g + 8)
                c_up, c_down, c_left, c_right, c_mix = [cf[i, part] for i in range(5)]
                d_up, d_down, d_left, d_right = [cf[i, part] for i in range(6, 10)]
                own = lev[part].astype(F32)
                sx, sy = out_flux[0, 2, part], out_flux[0, 3, part]
                col_low, col_high = crecv[s, ch, 0, part], crecv[s, ch, 1, part]

                def level(kk, held):
                    before, value, pack0, pack1 = held
                    k = first + kk
                    depth_here = k.astype(F32)
                    following = buf[slot, k + 1, rows]
                    up, down, left, right = sides(slot, k, kk, g, value, col_low, col_high)
                    fade = jnp.broadcast_to(dec[pl.ds(k, 1), :], (8, 128))
                    flow = (
                        jnp.where(depth_here < d_up, c_up * (up - value), 0.0)
                        + jnp.where(depth_here < d_down, c_down * (down - value), 0.0)
                        + jnp.where(depth_here < d_left, c_left * (left - value), 0.0)
                        + jnp.where(depth_here < d_right, c_right * (right - value), 0.0)
                    )
                    flow = flow + c_mix * (
                        jnp.where(depth_here + 1.0 < own, following - value, 0.0) + (before - value)
                    )
                    flow = flow - wide(fade, 2) * (sx * (down - up) + sy * (right - left))
                    new = value + jnp.where(depth_here < own, flow, 0.0)
                    buf[1 - slot, k, rows] = new
                    if not packed:
                        return value, following, pack0, pack1
                    here = lane == kk
                    pack0 = jnp.where(here, pack_high(new, kk), pack0)
                    pack1 = jnp.where(here, pack_low(new, kk), pack1)
                    if g == 7:
                        rsend[1, ch, 0, pl.ds(kk, 1)] = new[7:8]
                    if g == 0:
                        rsend[1, ch, 1, pl.ds(kk, 1)] = new[0:1]
                    return value, following, pack0, pack1

                zero = jnp.zeros((8, 128), F32)
                held = (
                    buf[slot, jnp.maximum(first + start - 1, 0), rows],
                    buf[slot, first + start, rows],
                    zero,
                    zero,
                )
                held = lax.fori_loop(start, stop, level, held)
                if packed:
                    csend[1, ch, 0, part] = held[2]
                    csend[1, ch, 1, part] = held[3]

        def ocean_count(ch):
            return jnp.minimum(CH, OLEV - ch * CH)

        def halos_arrived_ocean(s, ch):
            for copy in halo_copies(s, ch):
                copy.wait_recv()

        for copy in halo_copies(0, 0):
            copy.wait_recv()
        static_part()
        for at, other in enumerate(shifted(depth, 1)):
            cf[6 + at] = other
        def deep_step(t, carry):
            ch = NCH - 1 - t
            halos_arrived_ocean(0, ch)
            return carry

        lax.fori_loop(0, NCH - 1, deep_step, 0)

        def step0(t, carry):
            ch = NCH - 1 - t
            rows_in(0, 0, ch, CH)
            levels(0, ch, 0, ocean_count(ch), True)
            for copy in halo_copies(1, ch):
                copy.start()
            return carry

        lax.fori_loop(0, NCH, step0, 0)

        gain = surface * 4.0 * c2
        hand_over.wait_recv()
        qb[...] = buf[1, 0, TAB : TAB + CX] + gain * (hst[0] + 0.3 * hst[1])
        q_moves = (
            (qb.at[CX - 8 : CX], qrow.at[0], near(1, 0)),
            (qb.at[0:8], qrow.at[1], near(-1, 0)),
            (qb.at[:, 128:256], qcol.at[0], near(0, 1)),
            (qb.at[:, 0:128], qcol.at[1], near(0, -1)),
        )
        q_copies = [
            pltpu.make_async_remote_copy(
                src, dst, qs_sem.at[i], qr_sem.at[i], device_id=there, device_id_type=MESH
            )
            for i, (src, dst, there) in enumerate(q_moves)
        ]
        for copy in q_copies:
            copy.start()

        def step1(t, carry):
            ch = NCH - 1 - t
            halos_arrived_ocean(1, ch)
            rows_in(1, 1, ch, CH)
            levels(1, ch, jnp.where(ch == 0, 2, 0), ocean_count(ch), False)
            return carry

        lax.fori_loop(0, NCH, step1, 0)
        deep = pltpu.make_async_copy(
            buf.at[0, pl.ds(2, LEV - 2), pl.ds(TAB, CX)], out_state.at[0, pl.ds(2, LEV - 2)], out_sem
        )
        deep.start()

        total = jnp.zeros((16, 128), F32)
        for d in range(8):
            along_tx(d).wait_recv()
            total = total + red2[d]
        fix = jnp.sum(total[0:8], keepdims=True) / jnp.maximum(jnp.sum(total[8:16], keepdims=True), 1.0)
        flux0 = surface * (hst[0] + fix)
        flux1 = surface * hst[1]
        out_flux[0, 0] = flux0
        out_flux[0, 1] = flux1
        buf[1, 0, TAB : TAB + CX] = qb[...] + gain * fix
        for copy in q_copies:
            copy.wait_recv()

        def gain_of(c2_edge, depth_edge):
            return (depth_edge > 0.0).astype(F32) * 4.0 * c2_edge

        for side, at, inner in ((0, TAB - 1, 7), (1, TAB + CX, 0)):
            edge = rrecv[0, 0, side]
            buf[1, 0, at : at + 1] = qrow[side, inner : inner + 1] + fix * gain_of(
                edge[CH + 2 : CH + 3], edge[CH + 1 : CH + 2]
            )
        low = gain_of(pltpu.roll(crecv[0, 0, 0], 128 - CH - 2, 1), pltpu.roll(crecv[0, 0, 0], 128 - CH - 1, 1))
        high = gain_of(pltpu.roll(crecv[0, 0, 1], 128 - CH - 2, 1), pltpu.roll(crecv[0, 0, 1], 128 - CH - 1, 1))
        lane_col = lax.broadcasted_iota(jnp.int32, (CX, 128), 1)
        crecv[1, 0, 0] = jnp.where(
            lane_col == 0, pltpu.roll(qcol[0], 1, 1) + fix * low, crecv[1, 0, 0]
        )
        crecv[1, 0, 1] = jnp.where(lane_col == 0, qcol[1] + fix * high, crecv[1, 0, 1])
        levels(1, 0, 0, 2, False)
        buf[0, 0, TAB : TAB + CX] = buf[0, 0, TAB : TAB + CX] + gain * (flux0 + 0.3 * flux1)
        shallow = pltpu.make_async_copy(
            buf.at[0, pl.ds(0, 2), pl.ds(TAB, CX)], out_state.at[0, pl.ds(0, 2)], in_sem.at[0]
        )
        shallow.start()
        for copy in q_copies:
            copy.wait_send()
        for ch in range(NCH):
            for copy in halo_copies(0, ch) + halo_copies(1, ch):
                copy.wait_send()
        deep.wait()
        shallow.wait()

    @pl.when(is_atm)
    def _():
        for s in range(3):
            for ch in range(NCH):
                for copy in halo_copies(s, ch):
                    copy.wait_send()

    for n in range(9):
        if n != 4:
            lnk_copy(n).wait_send()
            val_copy(n).wait_send()


def on_device(state, coeffs, forcing, levels, remap):
    vmem = pl.BlockSpec(memory_space=pltpu.VMEM)
    anywhere = pl.BlockSpec(memory_space=pl.ANY)
    dma = pltpu.SemaphoreType.DMA
    return pl.pallas_call(
        kernel,
        out_shape=(
            jax.ShapeDtypeStruct((1, LEV, CX, CY), F32),
            jax.ShapeDtypeStruct((1, 4, CX, CY), F32),
        ),
        in_specs=[anywhere, vmem, vmem, vmem, vmem],
        out_specs=(anywhere, vmem),
        scratch_shapes=[
            pltpu.VMEM((2, LEV, CX + 16, CY), F32),
            pltpu.VMEM((4, NCH, 2, 32, CY), F32),
            pltpu.VMEM((4, NCH, 2, CX, 128), F32),
            pltpu.VMEM((3, NCH, 2, 32, CY), F32),
            pltpu.VMEM((3, NCH, 2, CX, 128), F32),
            pltpu.VMEM((10, CX, CY), F32),
            pltpu.VMEM((9, 2, CAP), jnp.int32),
            pltpu.VMEM((9, 2, CAP), jnp.int32),
            pltpu.VMEM((9, 2, CAP), F32),
            pltpu.VMEM((9, 2, CAP), F32),
            pltpu.VMEM((5 * CX, CY), F32),
            pltpu.VMEM((4 * CX, CY), BF16),
            pltpu.VMEM((CY, 128), BF16),
            pltpu.VMEM((LEV, 128), F32),
            pltpu.VMEM((2, CX, CY), F32),
            pltpu.VMEM((2, CX, CY), F32),
            pltpu.VMEM((CX, CY), F32),
            pltpu.VMEM((2, 8, CY), F32),
            pltpu.VMEM((2, CX, 128), F32),
            pltpu.VMEM((16, 128), F32),
            pltpu.VMEM((8, 16, 128), F32),
            pltpu.VMEM((8, 16, 128), F32),
            dma((NCH,)),
            dma,
            dma((3, NCH, 4)),
            dma((3, NCH, 4)),
            dma((9,)),
            dma((9,)),
            dma((9,)),
            dma((9,)),
            dma,
            dma,
            dma((4,)),
            dma((4,)),
            dma((8,)),
            dma((8,)),
            dma((8,)),
            dma((8,)),
        ],
        compiler_params=pltpu.CompilerParams(
            collective_id=0, has_side_effects=True, vmem_limit_bytes=60 << 20
        ),
        name="window",
    )(state, coeffs, forcing, levels, remap)


def solution(mesh):
    return jax.shard_map(
        on_device,
        mesh=mesh,
        in_specs=(
            P("sec", None, "tx", "ty"),
            P("sec", None, "tx", "ty"),
            P(None, "tx", "ty"),
            P("tx", "ty"),
            P(None, ("tx", "ty")),
        ),
        out_specs=(P("sec", None, "tx", "ty"), P("sec", None, "tx", "ty")),
        check_vma=False,
    )
```

```python
import jax
import jax.numpy as jnp
from jax import lax
from jax.experimental import pallas as pl
from jax.experimental.pallas import tpu as pltpu
from jax.sharding import PartitionSpec as P

LEV, OLEV, CX, CY = 72, 60, 64, 256
CAP = 4096
TAB = 8
CH = 24
NCH = LEV // CH
STACK = 8
F32, BF16 = jnp.float32, jnp.bfloat16
MESH = pl.DeviceIdType.MESH


def hi_lo(x):
    high = x.astype(BF16)
    return high, (x - high.astype(F32)).astype(BF16)


def wide(x, count):
    return jnp.concatenate([x] * count, 1)


def kernel(
    state, coef, forc, lev, remap, out_state, out_flux,
    buf_a, buf_b, top, top2, rsend, csend, rrecv, crecv, ccomb, cf, lnk_s, lnk_r, val_s, val_r, acc, fb, iota,
    dec, rem, hst, qb, qrow, qcol, red, red1, red2,
    in_sem, out_sem, hs_sem, hr_sem, ls_sem, lr_sem, vs_sem, vr_sem, rs_sem, rr_sem,
    qs_sem, qr_sem, p1s_sem, p1r_sem, p2s_sem, p2r_sem,
):
    sec, tx, ty = lax.axis_index("sec"), lax.axis_index("tx"), lax.axis_index("ty")
    is_atm = sec == 0
    is_ocn = sec == 1

    def near(dx, dy):
        return (sec, lax.rem(tx + dx + 8, 8), lax.rem(ty + dy + 8, 8))

    barrier = pltpu.get_barrier_semaphore()
    for dx in (-1, 0, 1, 4):
        for dy in (-1, 0, 1):
            if dx != 0 or dy != 0:
                pl.semaphore_signal(barrier, 1, device_id=near(dx, dy), device_id_type=MESH)
    for dy in range(2, 7):
        pl.semaphore_signal(barrier, 1, device_id=near(0, dy), device_id_type=MESH)
    for dx in range(8):
        pl.semaphore_signal(
            barrier, 1, device_id=(1 - sec, lax.rem(tx + dx, 8), ty), device_id_type=MESH
        )

    def state_in(ch):
        return pltpu.make_async_copy(
            state.at[0, pl.ds(ch * CH, CH)],
            buf_a.at[pl.ds(ch * CH, CH), pl.ds(TAB, CX)],
            in_sem.at[ch],
        )

    for ch in range(NCH):
        state_in(ch).start()

    kap, mix, c2 = coef[0, 0], coef[0, 1], coef[0, 2]
    depth = jnp.where(is_atm, jnp.full((CX, CY), float(LEV), F32), lev[...].astype(F32))
    surface = (lev[...] > 0).astype(F32)

    def target_of(n):
        row_step = n // 3
        return near(row_step - 1 + 3 * (row_step // 2), n % 3 - 1)

    def lnk_copy(n):
        return pltpu.make_async_remote_copy(
            lnk_s.at[n], lnk_r.at[n], ls_sem.at[n], lr_sem.at[n],
            device_id=target_of(n), device_id_type=MESH,
        )

    def val_copy(n):
        return pltpu.make_async_remote_copy(
            val_s.at[n], val_r.at[n], vs_sem.at[n], vr_sem.at[n],
            device_id=target_of(n), device_id_type=MESH,
        )

    def halo_copies(s, ch):
        out = []
        for d, (there, low) in enumerate(
            ((near(1, 0), 0), (near(-1, 0), 1), (near(0, 1), 0), (near(0, -1), 1))
        ):
            source = rsend.at[s, ch, low] if d < 2 else csend.at[s, ch]
            recv = rrecv if d < 2 else crecv
            out.append(
                pltpu.make_async_remote_copy(
                    source, recv.at[s, ch, low], hs_sem.at[s, ch, d], hr_sem.at[s, ch, d],
                    device_id=there, device_id_type=MESH,
                )
            )
        return out

    def edge_copies():
        moves = (
            (qb.at[CX - 8 : CX], qrow.at[0], near(1, 0)),
            (qb.at[0:8], qrow.at[1], near(-1, 0)),
            (qb.at[:, 128:256], qcol.at[0], near(0, 1)),
            (qb.at[:, 0:128], qcol.at[1], near(0, -1)),
        )
        return [
            pltpu.make_async_remote_copy(
                source, there, qs_sem.at[i], qr_sem.at[i], device_id=device, device_id_type=MESH
            )
            for i, (source, there, device) in enumerate(moves)
        ]

    lane = lax.broadcasted_iota(jnp.int32, (8, 128), 1)
    lane3 = lax.broadcasted_iota(jnp.int32, (1, 8, 128), 2)
    lane_col = lax.broadcasted_iota(jnp.int32, (CX, 128), 1)

    def pack_edges(src, s, ch, extras=()):
        for g in range(8):
            packed = jnp.zeros((8, 128), F32)
            for i in range(CH + len(extras)):
                if i < CH:
                    both = src[ch * CH + i, TAB + 8 * g : TAB + 8 * g + 8]
                else:
                    both = extras[i - CH][8 * g : 8 * g + 8]
                ends = jnp.where(lane < 64, both[:, :128], both[:, 128:])
                packed = jnp.where((lane >> 1) == i, pltpu.roll(ends, 2 * i + 1, 1), packed)
            csend[s, ch, 8 * g : 8 * g + 8] = packed
        for i in range(0, CH, 8):
            rsend[s, ch, 0, i : i + 8] = src[pl.ds(ch * CH + i, 8), TAB + CX - 1]
            rsend[s, ch, 1, i : i + 8] = src[pl.ds(ch * CH + i, 8), TAB]
        for copy in halo_copies(s, ch):
            copy.start()

    def unpack_edges(src, s, ch):
        before, after = pltpu.roll(crecv[s, ch, 0], 1, 1), pltpu.roll(crecv[s, ch, 1], 127, 1)
        ccomb[...] = jnp.where((lane_col & 1) == 1, before, after)
        src[pl.ds(ch * CH, CH), TAB - 1] = rrecv[s, ch, 0, 0:CH]
        src[pl.ds(ch * CH, CH), TAB + CX] = rrecv[s, ch, 1, 0:CH]

    def halo_wait(s, ch):
        for copy in halo_copies(s, ch):
            copy.wait_recv()

    def sides(value, ends):
        first, last = value[:, :, :128], value[:, :, 128:]
        right_a, right_b = pltpu.roll(first, 1, 2), pltpu.roll(last, 1, 2)
        left_a, left_b = pltpu.roll(first, 127, 2), pltpu.roll(last, 127, 2)
        left = jnp.concatenate(
            [jnp.where(lane3 == 0, ends, right_a), jnp.where(lane3 == 0, right_a, right_b)], 2
        )
        right = jnp.concatenate(
            [jnp.where(lane3 == 127, left_b, left_a), jnp.where(lane3 == 127, ends, left_b)], 2
        )
        return left, right

    def ends_of(part, i, count):
        columns = ccomb[part]
        return jnp.concatenate(
            [pltpu.roll(columns, lax.rem(255 - 2 * (i + j), 128), 1)[None] for j in range(count)], 0
        )

    def atm_batch(src, dst, k, count, ends, g):
        part, at = slice(8 * g, 8 * g + 8), TAB + 8 * g
        c_up, c_down, c_left, c_right, c_mix, c_own = [cf[i, part][None] for i in range(6)]
        value = src[pl.ds(k, count), at : at + 8]
        before = src[pl.ds(jnp.maximum(k - 1, 0), 1), at : at + 8]
        after = src[pl.ds(jnp.minimum(k + count, LEV - 1), 1), at : at + 8]
        if count > 1:
            before = jnp.concatenate([before, value[:-1]], 0)
            after = jnp.concatenate([value[1:], after], 0)
        up = src[pl.ds(k, count), at - 1 : at + 7]
        down = src[pl.ds(k, count), at + 1 : at + 9]
        left, right = sides(value, ends)
        new = c_own * value + c_mix * (before + after)
        dst[pl.ds(k, count), at : at + 8] = (
            new + (c_up * up + c_down * down) + (c_left * left + c_right * right)
        )

    def cool(src, dst):
        rows = slice(TAB, TAB + CX)
        dst[0, rows] = dst[0, rows] - coef[0, 2] * (src[0, rows] - forc[3])

    def atm_chunk(src, dst, s, ch, wait=True):
        if wait:
            halo_wait(s, ch)
        unpack_edges(src, s, ch)

        def batch(b, carry):
            for g in range(8):
                ends = ends_of(slice(8 * g, 8 * g + 8), b * STACK, STACK)
                atm_batch(src, dst, ch * CH + b * STACK, STACK, ends, g)
            return carry

        lax.fori_loop(0, CH // STACK, batch, 0)
        if isinstance(ch, int):
            if ch == 0:
                cool(src, dst)
        else:
            pl.when(ch == 0)(lambda: cool(src, dst))
        if s < 2:
            pack_edges(dst, s + 1, ch)

    lane_all = lax.broadcasted_iota(jnp.int32, (CX, CY), 1)

    def around(plane, at):
        low_row = rrecv[0, 0, 0, CH + at : CH + at + 1]
        high_row = rrecv[0, 0, 1, CH + at : CH + at + 1]
        low_col = crecv[0, 0, 0][:, 2 * (CH + at) : 2 * (CH + at) + 1]
        high_col = crecv[0, 0, 1][:, 2 * (CH + at) + 1 : 2 * (CH + at) + 2]
        return (
            jnp.concatenate([low_row, plane[:-1]], 0),
            jnp.concatenate([plane[1:], high_row], 0),
            jnp.where(lane_all == 0, low_col, pltpu.roll(plane, 1, 1)),
            jnp.where(lane_all == CY - 1, high_col, pltpu.roll(plane, CY - 1, 1)),
        )

    def coefficients():
        total = jnp.zeros((CX, CY), F32)
        for at, other in enumerate(around(kap, 0)):
            half = 0.5 * (kap + other)
            cf[at] = half
            total = total + half
        cf[4] = mix
        cf[5] = (1.0 - total) - 2.0 * mix
        for at, other in enumerate(around(depth, 1)):
            cf[6 + at] = other

    pl.semaphore_wait(barrier, 24)
    for side, row in ((0, CX - 1), (1, 0)):
        rsend[0, 0, side, CH : CH + 8] = jnp.zeros((8, CY), F32)
        for at, plane in enumerate((kap, depth, c2)):
            rsend[0, 0, side, CH + at : CH + at + 1] = plane[row : row + 1]
    state_in(0).wait()
    pack_edges(buf_a, 0, 0, (kap, depth, c2))

    def more(ch, carry):
        state_in(ch).wait()
        pack_edges(buf_a, 0, ch)
        return carry

    lax.fori_loop(1, NCH, more, 0)
    for n in range(9):
        lnk_s[n] = remap[3:5, n * CAP : (n + 1) * CAP]
        if n != 4:
            lnk_copy(n).start()
    iota[...] = lax.broadcasted_iota(jnp.int32, (CY, 128), 0).astype(F32).astype(BF16)

    speed = 0.2 * jnp.sqrt(1.0 + forc[0] * forc[0] + forc[1] * forc[1])

    @pl.when(is_atm)
    def _():
        halo_wait(0, 0)
        coefficients()
        atm_chunk(buf_a, buf_b, 0, 0, False)
        atm_chunk(buf_a, buf_b, 0, 1)
        halo_wait(1, 0)
        unpack_edges(buf_b, 1, 0)
        for g in range(8):
            part = slice(8 * g, 8 * g + 8)
            atm_batch(buf_b, top, 0, 2, ends_of(part, 0, 2), g)
        cool(buf_b, top)
        qb[...] = top[0, TAB : TAB + CX]
        for copy in edge_copies():
            copy.start()
        atm_chunk(buf_a, buf_b, 0, 2)
        for copy in edge_copies():
            copy.wait_recv()
        top[0, TAB - 1 : TAB] = qrow[0, 7:8]
        top[0, TAB + CX : TAB + CX + 1] = qrow[1, 0:1]
        for g in range(8):
            part = slice(8 * g, 8 * g + 8)
            ends = jnp.where(lane == 0, pltpu.roll(qcol[0, part], 1, 1), pltpu.roll(qcol[1, part], 127, 1))
            atm_batch(top, top2, 0, 1, ends[None], g)
        cool(top, top2)
        heat = c2 * (top2[0, TAB : TAB + CX] - forc[3])
        out_flux[0, 0] = heat
        out_flux[0, 1] = forc[2] - 0.5 * heat
        out_flux[0, 2] = speed * forc[0]
        out_flux[0, 3] = speed * forc[1]

    @pl.when(is_ocn)
    def _():
        out_flux[0, 0] = speed * forc[0]
        out_flux[0, 1] = speed * forc[1]

    for c in range(2):
        high, low = hi_lo(out_flux[0, c])
        fb[CX * c : CX * (c + 1)] = high
        fb[2 * CX + CX * c : 2 * CX + CX * (c + 1)] = low
    one, none = jnp.array(1, BF16), jnp.array(0, BF16)

    def pick(t, carry):
        n = lax.rem(t + 5, 9)
        at = pl.multiple_of(n * CAP, CAP)
        source = remap[0:1, pl.ds(at, CAP)]
        weight = remap[4:5, pl.ds(at, CAP)].astype(F32)
        col = (source & (CY - 1)).astype(F32).astype(BF16)
        hot = jnp.where(wide(iota[...], CAP // 128) == col, one, none)
        product = jnp.dot(fb[...], hot, preferred_element_type=F32)
        here = lax.broadcasted_iota(jnp.int32, (CX, CAP), 0) == (source >> 8)
        for c in range(2):
            both = product[CX * c : CX * (c + 1)] + product[2 * CX + CX * c : 2 * CX + CX * (c + 1)]
            val_s[n, c : c + 1] = jnp.sum(jnp.where(here, both, 0.0), 0, keepdims=True) * weight

        @pl.when(n != 4)
        def _():
            val_copy(n).start()

        return carry

    lax.fori_loop(0, 9, pick, 0)
    lnk_r[4] = lnk_s[4]
    val_r[4] = val_s[4]
    acc[...] = jnp.zeros_like(acc)

    def add(t, carry):
        n = lax.rem(t + 4, 9)

        @pl.when(n != 4)
        def _():
            lnk_copy(n).wait_recv()
            val_copy(n).wait_recv()

        target = lnk_r[n, 0:1]
        weight = lnk_r[n, 1:2].astype(F32).astype(BF16)
        col = (target & (CY - 1)).astype(F32).astype(BF16)
        row = (target >> 8).astype(F32).astype(BF16)
        index = wide(iota[...], CAP // 128)
        hot = jnp.where(index == col, one, none)
        here = index[:CX] == row
        high0, low0 = hi_lo(val_r[n, 0:1])
        high1, low1 = hi_lo(val_r[n, 1:2])
        spread = jnp.concatenate(
            [jnp.where(here, x, none) for x in (high0, high1, low0, low1, weight)], 0
        )
        acc[...] += lax.dot_general(
            spread, hot, (((1,), (1,)), ((), ())), preferred_element_type=F32
        )
        return carry

    lax.fori_loop(0, 9, add, 0)
    per = 1.0 / jnp.maximum(acc[4 * CX : 5 * CX], 1.0)
    rem[0] = (acc[0:CX] + acc[2 * CX : 3 * CX]) * per
    rem[1] = (acc[CX : 2 * CX] + acc[3 * CX : 4 * CX]) * per

    hand_over = pltpu.make_async_remote_copy(
        rem, hst, rs_sem, rr_sem, device_id=(1 - sec, tx, ty), device_id_type=MESH
    )

    def along_ty(d):
        return pltpu.make_async_remote_copy(
            red, red1.at[d], p1s_sem.at[d], p1r_sem.at[d],
            device_id=near(0, d), device_id_type=MESH,
        )

    def along_tx(d):
        return pltpu.make_async_remote_copy(
            red1.at[0], red2.at[d], p2s_sem.at[d], p2r_sem.at[d],
            device_id=(1 - sec, lax.rem(tx + d, 8), ty), device_id_type=MESH,
        )

    def folded(plane):
        total = plane[0:8]
        for g in range(1, 8):
            total = total + plane[8 * g : 8 * g + 8]
        return total[:, :128] + total[:, 128:]

    def state_out(src, ch):
        return pltpu.make_async_copy(
            src.at[pl.ds(ch * CH, CH), pl.ds(TAB, CX)],
            out_state.at[0, pl.ds(ch * CH, CH)],
            out_sem.at[ch],
        )

    @pl.when(is_atm)
    def _():
        hand_over.start()
        red[0:8] = folded(out_flux[0, 0] - surface * rem[0])
        red[8:16] = folded(surface)
        for d in range(1, 8):
            along_ty(d).start()
        atm_chunk(buf_b, buf_a, 1, 0, False)
        total = red[...]
        for d in range(1, 8):
            along_ty(d).wait_recv()
            total = total + red1[d]
        red1[0] = total
        for d in range(8):
            along_tx(d).start()

        def second(ch, carry):
            atm_chunk(buf_b, buf_a, 1, ch)
            return carry

        lax.fori_loop(1, NCH, second, 0)

        def third(ch, carry):
            atm_chunk(buf_a, buf_b, 2, ch)
            state_out(buf_b, ch).start()
            return carry

        lax.fori_loop(0, NCH, third, 0)
        for d in range(1, 8):
            along_ty(d).wait_send()
        for d in range(8):
            along_tx(d).wait_send()
        hand_over.wait_send()
        for s in range(3):
            for ch in range(NCH):
                for copy in halo_copies(s, ch):
                    copy.wait_send()
        for ch in range(NCH):
            state_out(buf_b, ch).wait()

    @pl.when(is_ocn)
    def _():
        out_flux[0, 2] = surface * rem[0]
        out_flux[0, 3] = surface * rem[1]
        level8 = lax.broadcasted_iota(jnp.int32, (LEV, 8, 128), 0).astype(F32)
        dec[...] = 0.5 * jnp.exp(level8 * (-1 / 8))
        halo_wait(0, 0)
        coefficients()

        def ocn_batch(src, dst, k, count, ends, g):
            part, at = slice(8 * g, 8 * g + 8), TAB + 8 * g
            c_up, c_down, c_left, c_right, c_mix = [cf[i, part][None] for i in range(5)]
            d_up, d_down, d_left, d_right = [cf[i, part][None] for i in range(6, 10)]
            own = lev[part].astype(F32)[None]
            sx, sy = out_flux[0, 2, part][None], out_flux[0, 3, part][None]
            here = (lax.broadcasted_iota(jnp.int32, (count, 8, CY), 0) + k).astype(F32)
            fade = dec[pl.ds(k, count)]
            value = src[pl.ds(k, count), at : at + 8]
            before = src[pl.ds(jnp.maximum(k - 1, 0), 1), at : at + 8]
            after = src[pl.ds(k + count, 1), at : at + 8]
            before = jnp.concatenate([before, value[:-1]], 0)
            after = jnp.concatenate([value[1:], after], 0)
            up = src[pl.ds(k, count), at - 1 : at + 7]
            down = src[pl.ds(k, count), at + 1 : at + 9]
            left, right = sides(value, ends)
            flow = (
                jnp.where(here < d_up, c_up * (up - value), 0.0)
                + jnp.where(here < d_down, c_down * (down - value), 0.0)
                + jnp.where(here < d_left, c_left * (left - value), 0.0)
                + jnp.where(here < d_right, c_right * (right - value), 0.0)
            )
            flow = flow + c_mix * (
                jnp.where(here + 1.0 < own, after - value, 0.0) + (before - value)
            )
            flow = flow - jnp.concatenate([fade, fade], 2) * (sx * (down - up) + sy * (right - left))
            dst[pl.ds(k, count), at : at + 8] = value + jnp.where(here < own, flow, 0.0)

        def ocn_chunk(src, dst, s, ch):
            unpack_edges(src, s, ch)

            def batch(b, carry):
                for g in range(8):
                    ends = ends_of(slice(8 * g, 8 * g + 8), b * STACK, STACK)
                    ocn_batch(src, dst, ch * CH + b * STACK, STACK, ends, g)
                return carry

            batches = jnp.minimum(CH, OLEV - ch * CH + STACK - 1) // STACK
            lax.fori_loop(0, batches, batch, 0)

        def first(ch, carry):
            @pl.when(ch > 0)
            def _():
                halo_wait(0, ch)

            ocn_chunk(buf_a, buf_b, 0, ch)
            pack_edges(buf_b, 1, ch)
            return carry

        lax.fori_loop(0, NCH, first, 0)

        def second(ch, carry):
            halo_wait(1, ch)
            ocn_chunk(buf_b, buf_a, 1, ch)

            @pl.when(ch > 0)
            def _():
                state_out(buf_a, ch).start()

            return carry

        lax.fori_loop(0, NCH, second, 0)
        deep = pltpu.make_async_copy(
            buf_a.at[pl.ds(2, CH - 2), pl.ds(TAB, CX)], out_state.at[0, pl.ds(2, CH - 2)], out_sem.at[0]
        )
        deep.start()

        gain = surface * 4.0 * c2
        hand_over.wait_recv()
        qb[...] = buf_b[0, TAB : TAB + CX] + gain * (hst[0] + 0.3 * hst[1])
        for copy in edge_copies():
            copy.start()

        total = jnp.zeros((16, 128), F32)
        for d in range(8):
            along_tx(d).wait_recv()
            total = total + red2[d]
        fix = jnp.sum(total[0:8], keepdims=True) / jnp.maximum(jnp.sum(total[8:16], keepdims=True), 1.0)
        flux0 = surface * (hst[0] + fix)
        flux1 = surface * hst[1]
        out_flux[0, 0] = flux0
        out_flux[0, 1] = flux1
        buf_b[0, TAB : TAB + CX] = qb[...] + gain * fix
        for copy in edge_copies():
            copy.wait_recv()

        def gain_of(c2_edge, depth_edge):
            return (depth_edge > 0.0).astype(F32) * 4.0 * c2_edge

        for side, at, inner in ((0, TAB - 1, 7), (1, TAB + CX, 0)):
            edge = rrecv[0, 0, side]
            buf_b[0, at : at + 1] = qrow[side, inner : inner + 1] + fix * gain_of(
                edge[CH + 2 : CH + 3], edge[CH + 1 : CH + 2]
            )
        lane_c2, lane_depth = 2 * (CH + 2), 2 * (CH + 1)
        low = gain_of(
            pltpu.roll(crecv[0, 0, 0], 128 - lane_c2, 1), pltpu.roll(crecv[0, 0, 0], 128 - lane_depth, 1)
        )
        high = gain_of(
            pltpu.roll(crecv[0, 0, 1], 126 - lane_c2, 1), pltpu.roll(crecv[0, 0, 1], 126 - lane_depth, 1)
        )
        surface_ends = jnp.where(
            lane_col == 0,
            pltpu.roll(qcol[0], 1, 1) + fix * low,
            pltpu.roll(qcol[1], 127, 1) + fix * high,
        )
        unpack_columns = pltpu.roll(crecv[1, 0, 0], 1, 1), pltpu.roll(crecv[1, 0, 1], 127, 1)
        ccomb[...] = jnp.where((lane_col & 1) == 1, unpack_columns[0], unpack_columns[1])
        for g in range(8):
            part = slice(8 * g, 8 * g + 8)
            ends = jnp.concatenate([surface_ends[part][None], ends_of(part, 1, 1)], 0)
            ocn_batch(buf_b, buf_a, 0, 2, ends, g)
        buf_a[0, TAB : TAB + CX] = buf_a[0, TAB : TAB + CX] + gain * (flux0 + 0.3 * flux1)
        shallow = pltpu.make_async_copy(
            buf_a.at[pl.ds(0, 2), pl.ds(TAB, CX)], out_state.at[0, pl.ds(0, 2)], in_sem.at[0]
        )
        shallow.start()
        for s in range(2):
            for ch in range(NCH):
                for copy in halo_copies(s, ch):
                    copy.wait_send()
        deep.wait()
        for ch in range(1, NCH):
            state_out(buf_a, ch).wait()
        shallow.wait()

    for copy in edge_copies():
        copy.wait_send()
    for n in range(9):
        if n != 4:
            lnk_copy(n).wait_send()
            val_copy(n).wait_send()


def on_device(state, coeffs, forcing, levels, remap):
    vmem = pl.BlockSpec(memory_space=pltpu.VMEM)
    anywhere = pl.BlockSpec(memory_space=pl.ANY)
    dma = pltpu.SemaphoreType.DMA
    return pl.pallas_call(
        kernel,
        out_shape=(
            jax.ShapeDtypeStruct((1, LEV, CX, CY), F32),
            jax.ShapeDtypeStruct((1, 4, CX, CY), F32),
        ),
        in_specs=[anywhere, vmem, vmem, vmem, vmem],
        out_specs=(anywhere, vmem),
        scratch_shapes=[
            pltpu.VMEM((LEV, CX + 16, CY), F32),
            pltpu.VMEM((LEV, CX + 16, CY), F32),
            pltpu.VMEM((2, CX + 16, CY), F32),
            pltpu.VMEM((2, CX + 16, CY), F32),
            pltpu.VMEM((3, NCH, 2, 32, CY), F32),
            pltpu.VMEM((3, NCH, CX, 128), F32),
            pltpu.VMEM((3, NCH, 2, 32, CY), F32),
            pltpu.VMEM((3, NCH, 2, CX, 128), F32),
            pltpu.VMEM((CX, 128), F32),
            pltpu.VMEM((10, CX, CY), F32),
            pltpu.VMEM((9, 2, CAP), jnp.int32),
            pltpu.VMEM((9, 2, CAP), jnp.int32),
            pltpu.VMEM((9, 2, CAP), F32),
            pltpu.VMEM((9, 2, CAP), F32),
            pltpu.VMEM((5 * CX, CY), F32),
            pltpu.VMEM((4 * CX, CY), BF16),
            pltpu.VMEM((CY, 128), BF16),
            pltpu.VMEM((LEV, 8, 128), F32),
            pltpu.VMEM((2, CX, CY), F32),
            pltpu.VMEM((2, CX, CY), F32),
            pltpu.VMEM((CX, CY), F32),
            pltpu.VMEM((2, 8, CY), F32),
            pltpu.VMEM((2, CX, 128), F32),
            pltpu.VMEM((16, 128), F32),
            pltpu.VMEM((8, 16, 128), F32),
            pltpu.VMEM((8, 16, 128), F32),
            dma((NCH,)),
            dma((NCH,)),
            dma((3, NCH, 4)),
            dma((3, NCH, 4)),
            dma((9,)),
            dma((9,)),
            dma((9,)),
            dma((9,)),
            dma,
            dma,
            dma((4,)),
            dma((4,)),
            dma((8,)),
            dma((8,)),
            dma((8,)),
            dma((8,)),
        ],
        compiler_params=pltpu.CompilerParams(
            collective_id=0, has_side_effects=True, vmem_limit_bytes=60 << 20
        ),
        name="window",
    )(state, coeffs, forcing, levels, remap)


def solution(mesh):
    return jax.shard_map(
        on_device,
        mesh=mesh,
        in_specs=(
            P("sec", None, "tx", "ty"),
            P("sec", None, "tx", "ty"),
            P(None, "tx", "ty"),
            P("tx", "ty"),
            P(None, ("tx", "ty")),
        ),
        out_specs=(P("sec", None, "tx", "ty"), P("sec", None, "tx", "ty")),
        check_vma=False,
    )
```

```python
import jax
import jax.numpy as jnp
from jax import lax
from jax.experimental import pallas as pl
from jax.experimental.pallas import tpu as pltpu
from jax.sharding import PartitionSpec as P

LEV, OLEV, CX, CY = 72, 60, 64, 256
CAP = 4096
TAB = 8
CH = 24
NCH = LEV // CH
STACK = 8
F32, BF16 = jnp.float32, jnp.bfloat16
MESH = pl.DeviceIdType.MESH


def hi_lo(x):
    high = x.astype(BF16)
    return high, (x - high.astype(F32)).astype(BF16)


def wide(x, count):
    return jnp.concatenate([x] * count, 1)


def kernel(
    state, coef_in, forc_in, lev_in, remap_in, out_state, out_flux,
    coef, forc, lev, remap, buf_a, buf_b, top, top2, rsend, csend, rrecv, crecv, ccomb, cf, lnk_s, lnk_r, val_s, val_r, acc, fb, iota,
    dec, rem, hst, per, qb, qcs, qrow, qcol, red, red1, red2,
    in_sem, hs_sem, hr_sem, ls_sem, lr_sem, fs_sem, fr_sem, ps_sem, pr_sem, vs_sem, vr_sem, rs_sem, rr_sem,
    qs_sem, qr_sem, p1s_sem, p1r_sem, p2s_sem, p2r_sem,
):
    sec, tx, ty = lax.axis_index("sec"), lax.axis_index("tx"), lax.axis_index("ty")
    is_atm = sec == 0
    is_ocn = sec == 1

    def near(dx, dy):
        return (sec, lax.rem(tx + dx + 8, 8), lax.rem(ty + dy + 8, 8))

    barrier = pltpu.get_barrier_semaphore()
    for dx in (-1, 0, 1, 4):
        for dy in (-1, 0, 1):
            if dx != 0 or dy != 0:
                pl.semaphore_signal(barrier, 1, device_id=near(dx, dy), device_id_type=MESH)
    for dy in range(2, 7):
        pl.semaphore_signal(barrier, 1, device_id=near(0, dy), device_id_type=MESH)
    for dx in range(8):
        pl.semaphore_signal(
            barrier, 1, device_id=(1 - sec, lax.rem(tx + dx, 8), ty), device_id_type=MESH
        )

    def state_in(ch):
        return pltpu.make_async_copy(
            state.at[0, pl.ds(ch * CH, CH)],
            buf_a.at[pl.ds(ch * CH, CH), pl.ds(TAB, CX)],
            in_sem.at[ch],
        )

    small_in = [
        pltpu.make_async_copy(source, there, in_sem.at[NCH + i])
        for i, (source, there) in enumerate(
            ((coef_in, coef), (lev_in, lev), (forc_in, forc), (remap_in, remap))
        )
    ]
    for copy in small_in[:3]:
        copy.start()
    state_in(0).start()
    small_in[3].start()
    for ch in range(1, NCH):
        state_in(ch).start()
    iota[...] = lax.broadcasted_iota(jnp.int32, (CY, 128), 0).astype(F32).astype(BF16)
    for copy in small_in[:3]:
        copy.wait()

    kap, mix, c2 = coef[0, 0], coef[0, 1], coef[0, 2]
    depth = jnp.where(is_atm, jnp.full((CX, CY), float(LEV), F32), lev[...].astype(F32))
    surface = (lev[...] > 0).astype(F32)

    def target_of(n):
        row_step = n // 3
        return near(row_step - 1 + 3 * (row_step // 2), n % 3 - 1)

    def lnk_copy(n):
        return pltpu.make_async_remote_copy(
            lnk_s.at[n], lnk_r.at[n], ls_sem.at[n], lr_sem.at[n],
            device_id=target_of(n), device_id_type=MESH,
        )

    def lnk_pass(n):
        return pltpu.make_async_remote_copy(
            lnk_r.at[n], lnk_r.at[n], fs_sem.at[n], fr_sem.at[n],
            device_id=(1 - sec, tx, ty), device_id_type=MESH,
        )

    def val_copy(n):
        return pltpu.make_async_remote_copy(
            val_s.at[n], val_r.at[n], vs_sem.at[n], vr_sem.at[n],
            device_id=target_of(n), device_id_type=MESH,
        )

    def halo_copies(s, ch):
        out = []
        for d, (there, low) in enumerate(
            ((near(1, 0), 0), (near(-1, 0), 1), (near(0, 1), 0), (near(0, -1), 1))
        ):
            if d < 2:
                count = CH + 8 if isinstance(ch, int) and (s, ch) == (0, 0) else CH
                source = rsend.at[s, ch, low, pl.ds(0, count)]
                recv = rrecv.at[s, ch, low, pl.ds(0, count)]
            else:
                source, recv = csend.at[s, ch, low], crecv.at[s, ch, low]
            out.append(
                pltpu.make_async_remote_copy(
                    source, recv, hs_sem.at[s, ch, d], hr_sem.at[s, ch, d],
                    device_id=there, device_id_type=MESH,
                )
            )
        return out

    def edge_copies():
        moves = (
            (qb.at[CX - 8 : CX], qrow.at[0], near(1, 0)),
            (qb.at[0:8], qrow.at[1], near(-1, 0)),
            (qcs.at[0], qcol.at[0], near(0, 1)),
            (qcs.at[1], qcol.at[1], near(0, -1)),
        )
        return [
            pltpu.make_async_remote_copy(
                source, there, qs_sem.at[i], qr_sem.at[i], device_id=device, device_id_type=MESH
            )
            for i, (source, there, device) in enumerate(moves)
        ]

    lane = lax.broadcasted_iota(jnp.int32, (8, 128), 1)
    lane3 = lax.broadcasted_iota(jnp.int32, (1, 8, 128), 2)

    def lanes_of(g):
        return 32 * (g % 4), slice(8 * (g // 4), 8 * (g // 4) + 8)

    def pack_pair(both, at, packed):
        ends = pltpu.roll(jnp.where(lane < 64, both[:, :128], both[:, 128:]), at + 1, 1)
        return jnp.where(lane == at, ends, packed[0]), jnp.where(lane == at + 1, ends, packed[1])

    def pack_edges(src, s, ch, extras=()):
        for q in range(2):
            packed = jnp.zeros((8, 128), F32), jnp.zeros((8, 128), F32)
            for g in range(4 * q, 4 * q + 4):
                base, part = lanes_of(g)
                for i in range(CH + len(extras)):
                    if i < CH:
                        both = src[ch * CH + i, TAB + 8 * g : TAB + 8 * g + 8]
                    else:
                        both = extras[i - CH][8 * g : 8 * g + 8]
                    packed = pack_pair(both, base + i, packed)
            csend[s, ch, 0, part] = packed[0]
            csend[s, ch, 1, part] = packed[1]
        for i in range(0, CH, 8):
            rsend[s, ch, 0, i : i + 8] = src[pl.ds(ch * CH + i, 8), TAB + CX - 1]
            rsend[s, ch, 1, i : i + 8] = src[pl.ds(ch * CH + i, 8), TAB]

    def halo_send(s, ch):
        for copy in halo_copies(s, ch):
            copy.start()

    def edge_send():
        packed = jnp.zeros((8, 128), F32), jnp.zeros((8, 128), F32)
        for g in range(8):
            packed = pack_pair(qb[8 * g : 8 * g + 8], g, packed)
        qcs[0], qcs[1] = packed
        for copy in edge_copies():
            copy.start()

    def unpack_columns(s, ch):
        ccomb[0] = crecv[s, ch, 0]
        ccomb[1] = pltpu.roll(crecv[s, ch, 1], 126, 1)

    def unpack_edges(src, s, ch):
        unpack_columns(s, ch)
        src[pl.ds(ch * CH, CH), TAB - 1] = rrecv[s, ch, 0, 0:CH]
        src[pl.ds(ch * CH, CH), TAB + CX] = rrecv[s, ch, 1, 0:CH]

    def halo_wait(s, ch):
        for copy in halo_copies(s, ch):
            copy.wait_recv()

    def sides(value, ends):
        first, last = value[:, :, :128], value[:, :, 128:]
        right_a, right_b = pltpu.roll(first, 1, 2), pltpu.roll(last, 1, 2)
        left_a, left_b = pltpu.roll(first, 127, 2), pltpu.roll(last, 127, 2)
        left = jnp.concatenate(
            [jnp.where(lane3 == 0, ends, right_a), jnp.where(lane3 == 0, right_a, right_b)], 2
        )
        right = jnp.concatenate(
            [jnp.where(lane3 == 127, left_b, left_a), jnp.where(lane3 == 127, ends, left_b)], 2
        )
        return left, right

    def ends_of(g, i, count):
        base, part = lanes_of(g)
        low, high = ccomb[0, part], ccomb[1, part]
        out = []
        for j in range(count):
            at = base + i + j
            out.append(pltpu.roll(jnp.where(lane == at, low, high), lax.rem(128 - at, 128), 1)[None])
        return jnp.concatenate(out, 0)

    def put(dst, k, count, g, value):
        if dst is out_state:
            out_state[0, pl.ds(k, count), 8 * g : 8 * g + 8] = value
        else:
            dst[pl.ds(k, count), TAB + 8 * g : TAB + 8 * g + 8] = value

    def atm_batch(src, dst, k, count, ends, g):
        part, at = slice(8 * g, 8 * g + 8), TAB + 8 * g
        c_up, c_down, c_left, c_right, c_mix, c_own = [cf[i, part][None] for i in range(6)]
        value = src[pl.ds(k, count), at : at + 8]
        before = src[pl.ds(jnp.maximum(k - 1, 0), 1), at : at + 8]
        after = src[pl.ds(jnp.minimum(k + count, LEV - 1), 1), at : at + 8]
        if count > 1:
            before = jnp.concatenate([before, value[:-1]], 0)
            after = jnp.concatenate([value[1:], after], 0)
        up = src[pl.ds(k, count), at - 1 : at + 7]
        down = src[pl.ds(k, count), at + 1 : at + 9]
        left, right = sides(value, ends)
        new = c_own * value + c_mix * (before + after)
        new = new + (c_up * up + c_down * down) + (c_left * left + c_right * right)
        put(dst, k, count, g, new)

    def cool(src, dst):
        rows = slice(TAB, TAB + CX)
        heat = coef[0, 2] * (src[0, rows] - forc[3])
        if dst is out_state:
            dst[0, 0] = dst[0, 0] - heat
        else:
            dst[0, rows] = dst[0, rows] - heat

    def atm_chunk(src, dst, s, ch, wait=True):
        if wait:
            halo_wait(s, ch)
        unpack_edges(src, s, ch)

        def batch(b, carry):
            for g in range(8):
                ends = ends_of(g, b * STACK, STACK)
                atm_batch(src, dst, ch * CH + b * STACK, STACK, ends, g)
            return carry

        lax.fori_loop(0, CH // STACK, batch, 0)
        if isinstance(ch, int):
            if ch == 0:
                cool(src, dst)
        else:
            pl.when(ch == 0)(lambda: cool(src, dst))
        if s < 2:
            pack_edges(dst, s + 1, ch)
            halo_send(s + 1, ch)

    lane_all = lax.broadcasted_iota(jnp.int32, (CX, CY), 1)

    def around(plane, at):
        low_row = rrecv[0, 0, 0, CH + at : CH + at + 1]
        high_row = rrecv[0, 0, 1, CH + at : CH + at + 1]
        low_col, high_col = [], []
        for g in range(8):
            base, part = lanes_of(g)
            low_col.append(crecv[0, 0, 0, part][:, base + CH + at : base + CH + at + 1])
            high_col.append(crecv[0, 0, 1, part][:, base + CH + at + 1 : base + CH + at + 2])
        low_col, high_col = jnp.concatenate(low_col, 0), jnp.concatenate(high_col, 0)
        return (
            jnp.concatenate([low_row, plane[:-1]], 0),
            jnp.concatenate([plane[1:], high_row], 0),
            jnp.where(lane_all == 0, low_col, pltpu.roll(plane, 1, 1)),
            jnp.where(lane_all == CY - 1, high_col, pltpu.roll(plane, CY - 1, 1)),
        )

    def coefficients():
        total = jnp.zeros((CX, CY), F32)
        for at, other in enumerate(around(kap, 0)):
            half = 0.5 * (kap + other)
            cf[at] = half
            total = total + half
        cf[4] = mix
        cf[5] = (1.0 - total) - 2.0 * mix
        for at, other in enumerate(around(depth, 1)):
            cf[6 + at] = other

    def first_halos():
        for side, row in ((0, CX - 1), (1, 0)):
            rsend[0, 0, side, CH : CH + 8] = jnp.zeros((8, CY), F32)
            for at, plane in enumerate((kap, depth, c2)):
                rsend[0, 0, side, CH + at : CH + at + 1] = plane[row : row + 1]
        state_in(0).wait()
        pack_edges(buf_a, 0, 0, (kap, depth, c2))

    def other_halos():
        def more(ch, carry):
            state_in(ch).wait()
            pack_edges(buf_a, 0, ch)
            halo_send(0, ch)
            return carry

        lax.fori_loop(1, NCH, more, 0)

    pl.when(is_atm)(first_halos)

    def stage_links():
        small_in[3].wait()
        for n in range(9):
            lnk_s[n] = remap[3:5, n * CAP : (n + 1) * CAP]

    pl.when(is_ocn)(stage_links)
    pl.semaphore_wait(barrier, 24)

    speed = 0.2 * jnp.sqrt(1.0 + forc[0] * forc[0] + forc[1] * forc[1])

    @pl.when(is_atm)
    def _():
        halo_send(0, 0)
        other_halos()
        stage_links()
        halo_wait(0, 0)
        coefficients()
        atm_chunk(buf_a, buf_b, 0, 0, False)
        atm_chunk(buf_a, buf_b, 0, 1)
        halo_wait(1, 0)
        unpack_edges(buf_b, 1, 0)
        for g in range(8):
            atm_batch(buf_b, top, 0, 2, ends_of(g, 0, 2), g)
        cool(buf_b, top)
        qb[...] = top[0, TAB : TAB + CX]
        edge_send()
        atm_chunk(buf_a, buf_b, 0, 2)
        for copy in edge_copies():
            copy.wait_recv()
        top[0, TAB - 1 : TAB] = qrow[0, 7:8]
        top[0, TAB + CX : TAB + CX + 1] = qrow[1, 0:1]
        for g in range(8):
            ends = jnp.where(lane == 0, pltpu.roll(qcol[0], (128 - g) % 128, 1), pltpu.roll(qcol[1], 126 - g, 1))
            atm_batch(top, top2, 0, 1, ends[None], g)
        cool(top, top2)
        heat = c2 * (top2[0, TAB : TAB + CX] - forc[3])
        out_flux[0, 0] = heat
        out_flux[0, 1] = forc[2] - 0.5 * heat
        out_flux[0, 2] = speed * forc[0]
        out_flux[0, 3] = speed * forc[1]

    @pl.when(is_ocn)
    def _():
        for n in range(9):
            if n != 4:
                lnk_copy(n).start()
        out_flux[0, 0] = speed * forc[0]
        out_flux[0, 1] = speed * forc[1]

    for c in range(2):
        high, low = hi_lo(out_flux[0, c])
        fb[CX * c : CX * (c + 1)] = high
        fb[2 * CX + CX * c : 2 * CX + CX * (c + 1)] = low
    one, none = jnp.array(1, BF16), jnp.array(0, BF16)

    def pick(t, carry):
        n = lax.rem(t + 5, 9)
        at = pl.multiple_of(n * CAP, CAP)
        source = remap[0:1, pl.ds(at, CAP)]
        weight = remap[4:5, pl.ds(at, CAP)].astype(F32)
        col = (source & (CY - 1)).astype(F32).astype(BF16)
        hot = jnp.where(wide(iota[...], CAP // 128) == col, one, none)
        product = jnp.dot(fb[...], hot, preferred_element_type=F32)
        here = lax.broadcasted_iota(jnp.int32, (CX, CAP), 0) == (source >> 8)
        for c in range(2):
            both = product[CX * c : CX * (c + 1)] + product[2 * CX + CX * c : 2 * CX + CX * (c + 1)]
            val_s[n, c : c + 1] = jnp.sum(jnp.where(here, both, 0.0), 0, keepdims=True) * weight

        @pl.when(n != 4)
        def _():
            val_copy(n).start()

        return carry

    lax.fori_loop(0, 9, pick, 0)
    lnk_r[4] = lnk_s[4]
    val_r[4] = val_s[4]
    acc[...] = jnp.zeros_like(acc)

    def add(t, arrived, fields):
        n = lax.rem(t + 4, 9)
        pl.when(n != 4)(lambda: arrived(n))
        target = lnk_r[n, 0:1]
        weight = lnk_r[n, 1:2].astype(F32).astype(BF16)
        col = (target & (CY - 1)).astype(F32).astype(BF16)
        row = (target >> 8).astype(F32).astype(BF16)
        index = wide(iota[...], CAP // 128)
        hot = jnp.where(index == col, one, none)
        here = index[:CX] == row
        high0, low0 = hi_lo(val_r[n, 0:1])
        high1, low1 = hi_lo(val_r[n, 1:2])
        spread = jnp.concatenate(
            [jnp.where(here, x, none) for x in (high0, high1, low0, low1, weight)[:fields]], 0
        )
        acc[0 : fields * CX] += lax.dot_general(
            spread, hot, (((1,), (1,)), ((), ())), preferred_element_type=F32
        )

    per_copy = pltpu.make_async_remote_copy(
        per.at[0], per.at[1], ps_sem, pr_sem, device_id=(1 - sec, tx, ty), device_id_type=MESH
    )

    @pl.when(is_atm)
    def _():
        def arrived(n):
            lnk_pass(n).wait_recv()
            val_copy(n).wait_recv()

        def step(t, carry):
            add(t, arrived, 4)
            return carry

        lax.fori_loop(0, 9, step, 0)
        per_copy.wait_recv()

    @pl.when(is_ocn)
    def _():
        first_halos()
        halo_send(0, 0)
        other_halos()
        for n in range(9):
            if n != 4:
                lnk_copy(n).wait_recv()
                lnk_pass(n).start()

        def step(t, carry):
            add(t, lambda n: val_copy(n).wait_recv(), 5)
            return carry

        lax.fori_loop(0, 9, step, 0)
        per[0] = 1.0 / jnp.maximum(acc[4 * CX : 5 * CX], 1.0)
        per_copy.start()
        per[1] = per[0]

    rem[0] = (acc[0:CX] + acc[2 * CX : 3 * CX]) * per[1]
    rem[1] = (acc[CX : 2 * CX] + acc[3 * CX : 4 * CX]) * per[1]

    hand_over = pltpu.make_async_remote_copy(
        rem, hst, rs_sem, rr_sem, device_id=(1 - sec, tx, ty), device_id_type=MESH
    )

    def along_ty(d):
        return pltpu.make_async_remote_copy(
            red, red1.at[d], p1s_sem.at[d], p1r_sem.at[d],
            device_id=near(0, d), device_id_type=MESH,
        )

    def along_tx(d):
        return pltpu.make_async_remote_copy(
            red1.at[0], red2.at[d], p2s_sem.at[d], p2r_sem.at[d],
            device_id=(1 - sec, lax.rem(tx + d, 8), ty), device_id_type=MESH,
        )

    def folded(plane):
        total = plane[0:8]
        for g in range(1, 8):
            total = total + plane[8 * g : 8 * g + 8]
        return total[:, :128] + total[:, 128:]

    @pl.when(is_atm)
    def _():
        hand_over.start()
        red[0:8] = folded(out_flux[0, 0] - surface * rem[0])
        red[8:16] = folded(surface)
        for d in range(1, 8):
            along_ty(d).start()
        atm_chunk(buf_b, buf_a, 1, 0, False)
        total = red[...]
        for d in range(1, 8):
            along_ty(d).wait_recv()
            total = total + red1[d]
        red1[0] = total
        for d in range(8):
            along_tx(d).start()

        def second(ch, carry):
            atm_chunk(buf_b, buf_a, 1, ch)
            return carry

        lax.fori_loop(1, NCH, second, 0)

        def third(ch, carry):
            atm_chunk(buf_a, out_state, 2, ch)
            return carry

        lax.fori_loop(0, NCH, third, 0)
        for d in range(1, 8):
            along_ty(d).wait_send()
        for d in range(8):
            along_tx(d).wait_send()
        hand_over.wait_send()
        for s in range(3):
            for ch in range(NCH):
                for copy in halo_copies(s, ch):
                    copy.wait_send()

    @pl.when(is_ocn)
    def _():
        out_flux[0, 2] = surface * rem[0]
        out_flux[0, 3] = surface * rem[1]
        level8 = lax.broadcasted_iota(jnp.int32, (LEV, 8, 128), 0).astype(F32)
        dec[...] = 0.5 * jnp.exp(level8 * (-1 / 8))
        halo_wait(0, 0)
        coefficients()

        out_state[0, OLEV + STACK // 2 : LEV] = buf_a[OLEV + STACK // 2 : LEV, TAB : TAB + CX]

        def ocn_batch(src, dst, k, count, ends, g):
            part, at = slice(8 * g, 8 * g + 8), TAB + 8 * g
            c_up, c_down, c_left, c_right, c_mix = [cf[i, part][None] for i in range(5)]
            d_up, d_down, d_left, d_right = [cf[i, part][None] for i in range(6, 10)]
            own = lev[part].astype(F32)[None]
            sx, sy = out_flux[0, 2, part][None], out_flux[0, 3, part][None]
            here = (lax.broadcasted_iota(jnp.int32, (count, 8, CY), 0) + k).astype(F32)
            fade = dec[pl.ds(k, count)]
            value = src[pl.ds(k, count), at : at + 8]
            before = src[pl.ds(jnp.maximum(k - 1, 0), 1), at : at + 8]
            after = src[pl.ds(k + count, 1), at : at + 8]
            before = jnp.concatenate([before, value[:-1]], 0)
            after = jnp.concatenate([value[1:], after], 0)
            up = src[pl.ds(k, count), at - 1 : at + 7]
            down = src[pl.ds(k, count), at + 1 : at + 9]
            left, right = sides(value, ends)
            flow = (
                jnp.where(here < d_up, c_up * (up - value), 0.0)
                + jnp.where(here < d_down, c_down * (down - value), 0.0)
                + jnp.where(here < d_left, c_left * (left - value), 0.0)
                + jnp.where(here < d_right, c_right * (right - value), 0.0)
            )
            flow = flow + c_mix * (
                jnp.where(here + 1.0 < own, after - value, 0.0) + (before - value)
            )
            flow = flow - jnp.concatenate([fade, fade], 2) * (sx * (down - up) + sy * (right - left))
            put(dst, k, count, g, value + jnp.where(here < own, flow, 0.0))

        def ocn_chunk(src, dst, s, ch):
            unpack_edges(src, s, ch)

            def batch(b, carry):
                for g in range(8):
                    ends = ends_of(g, b * STACK, STACK)
                    ocn_batch(src, dst, ch * CH + b * STACK, STACK, ends, g)
                return carry

            batches = jnp.minimum(CH, OLEV - ch * CH + STACK - 1) // STACK
            lax.fori_loop(0, batches, batch, 0)

        def first(ch, carry):
            @pl.when(ch > 0)
            def _():
                halo_wait(0, ch)

            ocn_chunk(buf_a, buf_b, 0, ch)
            pack_edges(buf_b, 1, ch)
            halo_send(1, ch)
            return carry

        lax.fori_loop(0, NCH, first, 0)

        def second(ch, carry):
            halo_wait(1, ch)
            ocn_chunk(buf_b, out_state, 1, ch)
            return carry

        lax.fori_loop(0, NCH, second, 0)

        gain = surface * 4.0 * c2
        hand_over.wait_recv()
        qb[...] = buf_b[0, TAB : TAB + CX] + gain * (hst[0] + 0.3 * hst[1])
        edge_send()

        total = jnp.zeros((16, 128), F32)
        for d in range(8):
            along_tx(d).wait_recv()
            total = total + red2[d]
        fix = jnp.sum(total[0:8], keepdims=True) / jnp.maximum(jnp.sum(total[8:16], keepdims=True), 1.0)
        flux0 = surface * (hst[0] + fix)
        flux1 = surface * hst[1]
        out_flux[0, 0] = flux0
        out_flux[0, 1] = flux1
        buf_b[0, TAB : TAB + CX] = qb[...] + gain * fix
        for copy in edge_copies():
            copy.wait_recv()

        def gain_of(c2_edge, depth_edge):
            return (depth_edge > 0.0).astype(F32) * 4.0 * c2_edge

        for side, at, inner in ((0, TAB - 1, 7), (1, TAB + CX, 0)):
            edge = rrecv[0, 0, side]
            buf_b[0, at : at + 1] = qrow[side, inner : inner + 1] + fix * gain_of(
                edge[CH + 2 : CH + 3], edge[CH + 1 : CH + 2]
            )
        unpack_columns(1, 0)
        for g in range(8):
            base, part = lanes_of(g)
            low, high = crecv[0, 0, 0, part], crecv[0, 0, 1, part]
            at_depth, at_c2 = base + CH + 1, base + CH + 2
            low = gain_of(pltpu.roll(low, 128 - at_c2, 1), pltpu.roll(low, 128 - at_depth, 1))
            high = gain_of(pltpu.roll(high, 126 - at_c2, 1), pltpu.roll(high, 126 - at_depth, 1))
            ends = jnp.where(
                lane == 0,
                pltpu.roll(qcol[0], (128 - g) % 128, 1) + fix * low,
                pltpu.roll(qcol[1], 126 - g, 1) + fix * high,
            )
            ends = jnp.concatenate([ends[None], ends_of(g, 1, 1)], 0)
            ocn_batch(buf_b, out_state, 0, 2, ends, g)
        out_state[0, 0] = out_state[0, 0] + gain * (flux0 + 0.3 * flux1)
        for s in range(2):
            for ch in range(NCH):
                for copy in halo_copies(s, ch):
                    copy.wait_send()
        per_copy.wait_send()
        for n in range(9):
            if n != 4:
                lnk_copy(n).wait_send()
                lnk_pass(n).wait_send()

    for copy in edge_copies():
        copy.wait_send()
    for n in range(9):
        if n != 4:
            val_copy(n).wait_send()


def write_out(mid, flux, out_state, out_flux, sem):
    copies = [
        pltpu.make_async_copy(mid.at[:, pl.ds(12 * i, 12)], out_state.at[:, pl.ds(12 * i, 12)], sem.at[i])
        for i in range(6)
    ] + [pltpu.make_async_copy(flux, out_flux, sem.at[6])]
    for copy in copies:
        copy.start()
    for copy in copies:
        copy.wait()


def on_device(state, coeffs, forcing, levels, remap):
    vmem = pl.BlockSpec(memory_space=pltpu.VMEM)
    anywhere = pl.BlockSpec(memory_space=pl.ANY)
    hbm = pl.BlockSpec(memory_space=pltpu.HBM)
    dma = pltpu.SemaphoreType.DMA
    mid, flux = pl.pallas_call(
        kernel,
        out_shape=(
            pltpu.VMEM((1, LEV, CX, CY), F32),
            pltpu.VMEM((1, 4, CX, CY), F32),
        ),
        in_specs=[hbm] * 5,
        out_specs=(vmem, vmem),
        scratch_shapes=[
            pltpu.VMEM((1, 3, CX, CY), F32),
            pltpu.VMEM((4, CX, CY), F32),
            pltpu.VMEM((CX, CY), jnp.int32),
            pltpu.VMEM((5, 9 * CAP), jnp.int32),
            pltpu.VMEM((LEV, CX + 16, CY), F32),
            pltpu.VMEM((LEV, CX + 16, CY), F32),
            pltpu.VMEM((2, CX + 16, CY), F32),
            pltpu.VMEM((2, CX + 16, CY), F32),
            pltpu.VMEM((3, NCH, 2, 32, CY), F32),
            pltpu.VMEM((3, NCH, 2, 16, 128), F32),
            pltpu.VMEM((3, NCH, 2, 32, CY), F32),
            pltpu.VMEM((3, NCH, 2, 16, 128), F32),
            pltpu.VMEM((2, 16, 128), F32),
            pltpu.VMEM((10, CX, CY), F32),
            pltpu.VMEM((9, 2, CAP), jnp.int32),
            pltpu.VMEM((9, 2, CAP), jnp.int32),
            pltpu.VMEM((9, 2, CAP), F32),
            pltpu.VMEM((9, 2, CAP), F32),
            pltpu.VMEM((5 * CX, CY), F32),
            pltpu.VMEM((4 * CX, CY), BF16),
            pltpu.VMEM((CY, 128), BF16),
            pltpu.VMEM((LEV, 8, 128), F32),
            pltpu.VMEM((2, CX, CY), F32),
            pltpu.VMEM((2, CX, CY), F32),
            pltpu.VMEM((2, CX, CY), F32),
            pltpu.VMEM((CX, CY), F32),
            pltpu.VMEM((2, 8, 128), F32),
            pltpu.VMEM((2, 8, CY), F32),
            pltpu.VMEM((2, 8, 128), F32),
            pltpu.VMEM((16, 128), F32),
            pltpu.VMEM((8, 16, 128), F32),
            pltpu.VMEM((8, 16, 128), F32),
            dma((NCH + 4,)),
            dma((3, NCH, 4)),
            dma((3, NCH, 4)),
            dma((9,)),
            dma((9,)),
            dma((9,)),
            dma((9,)),
            dma,
            dma,
            dma((9,)),
            dma((9,)),
            dma,
            dma,
            dma((4,)),
            dma((4,)),
            dma((8,)),
            dma((8,)),
            dma((8,)),
            dma((8,)),
        ],
        compiler_params=pltpu.CompilerParams(
            collective_id=0, has_side_effects=True, vmem_limit_bytes=59 << 20
        ),
        name="window",
    )(state, coeffs, forcing, levels, remap)
    return pl.pallas_call(
        write_out,
        out_shape=(
            jax.ShapeDtypeStruct((1, LEV, CX, CY), F32),
            jax.ShapeDtypeStruct((1, 4, CX, CY), F32),
        ),
        in_specs=[vmem, vmem],
        out_specs=(anywhere, anywhere),
        scratch_shapes=[dma((7,))],
        compiler_params=pltpu.CompilerParams(vmem_limit_bytes=4 << 20),
        name="write_out",
    )(mid, flux)


def solution(mesh):
    return jax.shard_map(
        on_device,
        mesh=mesh,
        in_specs=(
            P("sec", None, "tx", "ty"),
            P("sec", None, "tx", "ty"),
            P(None, "tx", "ty"),
            P("tx", "ty"),
            P(None, ("tx", "ty")),
        ),
        out_specs=(P("sec", None, "tx", "ty"), P("sec", None, "tx", "ty")),
        check_vma=False,
    )
```

```python
import jax
import jax.numpy as jnp
from jax import lax
from jax.experimental import pallas as pl
from jax.experimental.pallas import tpu as pltpu
from jax.sharding import PartitionSpec as P

LEV, OLEV, CX, CY = 72, 60, 64, 256
CAP = 4096
TAB = 8
CH = 24
NCH = LEV // CH
STACK = 6
F32, BF16 = jnp.float32, jnp.bfloat16
MESH = pl.DeviceIdType.MESH


def hi_lo(x):
    high = x.astype(BF16)
    return high, (x - high.astype(F32)).astype(BF16)


def wide(x, count):
    return jnp.concatenate([x] * count, 1)


def kernel(
    state, coef_in, forc_in, lev_in, remap_in, out_state, out_flux,
    coef, forc, lev, remap, buf_a, buf_b, top, top2, rsend, csend, rrecv, crecv, ccomb, cf, lnk_s, lnk_r, val_s, val_r, acc, fb, iota,
    dec, rem, hst, per, qb, qcs, qrow, qcol, red, red1, red2,
    in_sem, hs_sem, hr_sem, ls_sem, lr_sem, fs_sem, fr_sem, ps_sem, pr_sem, vs_sem, vr_sem, rs_sem, rr_sem,
    qs_sem, qr_sem, p1s_sem, p1r_sem, p2s_sem, p2r_sem,
):
    sec, tx, ty = lax.axis_index("sec"), lax.axis_index("tx"), lax.axis_index("ty")
    is_atm = sec == 0
    is_ocn = sec == 1

    def near(dx, dy):
        return (sec, lax.rem(tx + dx + 8, 8), lax.rem(ty + dy + 8, 8))

    barrier = pltpu.get_barrier_semaphore()
    for dx in (-1, 0, 1, 4):
        for dy in (-1, 0, 1):
            if dx != 0 or dy != 0:
                pl.semaphore_signal(barrier, 1, device_id=near(dx, dy), device_id_type=MESH)
    for dy in range(2, 7):
        pl.semaphore_signal(barrier, 1, device_id=near(0, dy), device_id_type=MESH)
    for dx in (2, 3, 5, 6):
        pl.semaphore_signal(barrier, 1, device_id=near(dx, 0), device_id_type=MESH)
    pl.semaphore_signal(barrier, 1, device_id=(1 - sec, tx, ty), device_id_type=MESH)

    def state_in(ch):
        return pltpu.make_async_copy(
            state.at[0, pl.ds(ch * CH, CH)],
            buf_a.at[pl.ds(ch * CH, CH), pl.ds(TAB, CX)],
            in_sem.at[ch],
        )

    small_in = [
        pltpu.make_async_copy(source, there, in_sem.at[NCH + i])
        for i, (source, there) in enumerate(
            ((coef_in, coef), (lev_in, lev), (forc_in, forc), (remap_in, remap))
        )
    ]
    for copy in small_in[:3]:
        copy.start()
    state_in(0).start()
    small_in[3].start()
    for ch in range(1, NCH):
        state_in(ch).start()
    iota[...] = lax.broadcasted_iota(jnp.int32, (CY, 128), 0).astype(F32).astype(BF16)
    for copy in small_in[:3]:
        copy.wait()

    kap, mix, c2 = coef[0, 0], coef[0, 1], coef[0, 2]
    depth = jnp.where(is_atm, jnp.full((CX, CY), float(LEV), F32), lev[...].astype(F32))
    surface = (lev[...] > 0).astype(F32)

    def target_of(n):
        row_step = n // 3
        return near(row_step - 1 + 3 * (row_step // 2), n % 3 - 1)

    def lnk_copy(n):
        return pltpu.make_async_remote_copy(
            lnk_s.at[n], lnk_r.at[n], ls_sem.at[n], lr_sem.at[n],
            device_id=target_of(n), device_id_type=MESH,
        )

    def lnk_pass(n):
        return pltpu.make_async_remote_copy(
            lnk_r.at[n], lnk_r.at[n], fs_sem.at[n], fr_sem.at[n],
            device_id=(1 - sec, tx, ty), device_id_type=MESH,
        )

    def val_copy(n):
        return pltpu.make_async_remote_copy(
            val_s.at[n], val_r.at[n], vs_sem.at[n], vr_sem.at[n],
            device_id=target_of(n), device_id_type=MESH,
        )

    def halo_copies(s, ch):
        out = []
        for d, (there, low) in enumerate(
            ((near(1, 0), 0), (near(-1, 0), 1), (near(0, 1), 0), (near(0, -1), 1))
        ):
            if d < 2:
                count = CH + 8 if isinstance(ch, int) and (s, ch) == (0, 0) else CH
                source = rsend.at[s, ch, low, pl.ds(0, count)]
                recv = rrecv.at[s, ch, low, pl.ds(0, count)]
            else:
                source, recv = csend.at[s, ch, low], crecv.at[s, ch, low]
            out.append(
                pltpu.make_async_remote_copy(
                    source, recv, hs_sem.at[s, ch, d], hr_sem.at[s, ch, d],
                    device_id=there, device_id_type=MESH,
                )
            )
        return out

    def edge_copies():
        moves = (
            (qb.at[CX - 8 : CX], qrow.at[0], near(1, 0)),
            (qb.at[0:8], qrow.at[1], near(-1, 0)),
            (qcs.at[0], qcol.at[0], near(0, 1)),
            (qcs.at[1], qcol.at[1], near(0, -1)),
        )
        return [
            pltpu.make_async_remote_copy(
                source, there, qs_sem.at[i], qr_sem.at[i], device_id=device, device_id_type=MESH
            )
            for i, (source, there, device) in enumerate(moves)
        ]

    lane = lax.broadcasted_iota(jnp.int32, (8, 128), 1)
    lane3 = lax.broadcasted_iota(jnp.int32, (1, 8, 128), 2)

    def lanes_of(g):
        return 32 * (g % 4), slice(8 * (g // 4), 8 * (g // 4) + 8)

    def pack_pair(both, at, packed):
        ends = pltpu.roll(jnp.where(lane < 64, both[:, :128], both[:, 128:]), at + 1, 1)
        return jnp.where(lane == at, ends, packed[0]), jnp.where(lane == at + 1, ends, packed[1])

    def pack_edges(src, s, ch, extras=()):
        for q in range(2):
            packed = jnp.zeros((8, 128), F32), jnp.zeros((8, 128), F32)
            for g in range(4 * q, 4 * q + 4):
                base, part = lanes_of(g)
                for i in range(CH + len(extras)):
                    if i < CH:
                        both = src[ch * CH + i, TAB + 8 * g : TAB + 8 * g + 8]
                    else:
                        both = extras[i - CH][8 * g : 8 * g + 8]
                    packed = pack_pair(both, base + i, packed)
            csend[s, ch, 0, part] = packed[0]
            csend[s, ch, 1, part] = packed[1]
        for i in range(0, CH, 8):
            rsend[s, ch, 0, i : i + 8] = src[pl.ds(ch * CH + i, 8), TAB + CX - 1]
            rsend[s, ch, 1, i : i + 8] = src[pl.ds(ch * CH + i, 8), TAB]

    def halo_send(s, ch):
        for copy in halo_copies(s, ch):
            copy.start()

    def edge_send():
        packed = jnp.zeros((8, 128), F32), jnp.zeros((8, 128), F32)
        for g in range(8):
            packed = pack_pair(qb[8 * g : 8 * g + 8], g, packed)
        qcs[0], qcs[1] = packed
        for copy in edge_copies():
            copy.start()

    def unpack_columns(s, ch):
        ccomb[0] = crecv[s, ch, 0]
        ccomb[1] = pltpu.roll(crecv[s, ch, 1], 126, 1)

    def unpack_edges(src, s, ch):
        unpack_columns(s, ch)
        src[pl.ds(ch * CH, CH), TAB - 1] = rrecv[s, ch, 0, 0:CH]
        src[pl.ds(ch * CH, CH), TAB + CX] = rrecv[s, ch, 1, 0:CH]

    def halo_wait(s, ch):
        for copy in halo_copies(s, ch):
            copy.wait_recv()

    def sides(value, ends):
        first, last = value[:, :, :128], value[:, :, 128:]
        right_a, right_b = pltpu.roll(first, 1, 2), pltpu.roll(last, 1, 2)
        left_a, left_b = pltpu.roll(first, 127, 2), pltpu.roll(last, 127, 2)
        left = jnp.concatenate(
            [jnp.where(lane3 == 0, ends, right_a), jnp.where(lane3 == 0, right_a, right_b)], 2
        )
        right = jnp.concatenate(
            [jnp.where(lane3 == 127, left_b, left_a), jnp.where(lane3 == 127, ends, left_b)], 2
        )
        return left, right

    def ends_of(g, i, count):
        base, part = lanes_of(g)
        low, high = ccomb[0, part], ccomb[1, part]
        out = []
        for j in range(count):
            at = base + i + j
            out.append(pltpu.roll(jnp.where(lane == at, low, high), lax.rem(128 - at, 128), 1)[None])
        return jnp.concatenate(out, 0)

    def put(dst, k, count, g, value):
        if dst is out_state:
            out_state[0, pl.ds(k, count), 8 * g : 8 * g + 8] = value
        else:
            dst[pl.ds(k, count), TAB + 8 * g : TAB + 8 * g + 8] = value

    def atm_batch(src, dst, k, count, ends, g):
        part, at = slice(8 * g, 8 * g + 8), TAB + 8 * g
        c_up, c_down, c_left, c_right, c_mix, c_own = [cf[i, part][None] for i in range(6)]
        value = src[pl.ds(k, count), at : at + 8]
        before = src[pl.ds(jnp.maximum(k - 1, 0), 1), at : at + 8]
        after = src[pl.ds(jnp.minimum(k + count, LEV - 1), 1), at : at + 8]
        if count > 1:
            before = jnp.concatenate([before, value[:-1]], 0)
            after = jnp.concatenate([value[1:], after], 0)
        up = src[pl.ds(k, count), at - 1 : at + 7]
        down = src[pl.ds(k, count), at + 1 : at + 9]
        left, right = sides(value, ends)
        new = c_own * value + c_mix * (before + after)
        new = new + (c_up * up + c_down * down) + (c_left * left + c_right * right)
        put(dst, k, count, g, new)

    def cool(src, dst):
        rows = slice(TAB, TAB + CX)
        heat = coef[0, 2] * (src[0, rows] - forc[3])
        if dst is out_state:
            dst[0, 0] = dst[0, 0] - heat
        else:
            dst[0, rows] = dst[0, rows] - heat

    def atm_chunk(src, dst, s, ch, wait=True):
        if wait:
            halo_wait(s, ch)
        unpack_edges(src, s, ch)

        def batch(b, carry):
            for g in range(8):
                ends = ends_of(g, b * STACK, STACK)
                atm_batch(src, dst, ch * CH + b * STACK, STACK, ends, g)
            return carry

        lax.fori_loop(0, CH // STACK, batch, 0)
        if isinstance(ch, int):
            if ch == 0:
                cool(src, dst)
        else:
            pl.when(ch == 0)(lambda: cool(src, dst))
        if s < 2:
            pack_edges(dst, s + 1, ch)
            halo_send(s + 1, ch)

    lane_all = lax.broadcasted_iota(jnp.int32, (CX, CY), 1)

    def around(plane, at):
        low_row = rrecv[0, 0, 0, CH + at : CH + at + 1]
        high_row = rrecv[0, 0, 1, CH + at : CH + at + 1]
        low_col, high_col = [], []
        for g in range(8):
            base, part = lanes_of(g)
            low_col.append(crecv[0, 0, 0, part][:, base + CH + at : base + CH + at + 1])
            high_col.append(crecv[0, 0, 1, part][:, base + CH + at + 1 : base + CH + at + 2])
        low_col, high_col = jnp.concatenate(low_col, 0), jnp.concatenate(high_col, 0)
        return (
            jnp.concatenate([low_row, plane[:-1]], 0),
            jnp.concatenate([plane[1:], high_row], 0),
            jnp.where(lane_all == 0, low_col, pltpu.roll(plane, 1, 1)),
            jnp.where(lane_all == CY - 1, high_col, pltpu.roll(plane, CY - 1, 1)),
        )

    def coefficients():
        total = jnp.zeros((CX, CY), F32)
        for at, other in enumerate(around(kap, 0)):
            half = 0.5 * (kap + other)
            cf[at] = half
            total = total + half
        cf[4] = mix
        cf[5] = (1.0 - total) - 2.0 * mix
        for at, other in enumerate(around(depth, 1)):
            cf[6 + at] = other

    def first_halos():
        for side, row in ((0, CX - 1), (1, 0)):
            rsend[0, 0, side, CH : CH + 8] = jnp.zeros((8, CY), F32)
            for at, plane in enumerate((kap, depth, c2)):
                rsend[0, 0, side, CH + at : CH + at + 1] = plane[row : row + 1]
        state_in(0).wait()
        pack_edges(buf_a, 0, 0, (kap, depth, c2))

    def other_halos():
        def more(ch, carry):
            state_in(ch).wait()
            pack_edges(buf_a, 0, ch)
            halo_send(0, ch)
            return carry

        lax.fori_loop(1, NCH, more, 0)

    pl.when(is_atm)(first_halos)

    def stage_links():
        small_in[3].wait()
        for n in range(9):
            lnk_s[n] = remap[3:5, n * CAP : (n + 1) * CAP]

    pl.when(is_ocn)(stage_links)
    pl.semaphore_wait(barrier, 21)

    speed = 0.2 * jnp.sqrt(1.0 + forc[0] * forc[0] + forc[1] * forc[1])

    @pl.when(is_atm)
    def _():
        halo_send(0, 0)
        other_halos()
        stage_links()
        halo_wait(0, 0)
        coefficients()
        atm_chunk(buf_a, buf_b, 0, 0, False)
        atm_chunk(buf_a, buf_b, 0, 1)
        halo_wait(1, 0)
        unpack_edges(buf_b, 1, 0)
        for g in range(8):
            atm_batch(buf_b, top, 0, 2, ends_of(g, 0, 2), g)
        cool(buf_b, top)
        qb[...] = top[0, TAB : TAB + CX]
        edge_send()
        atm_chunk(buf_a, buf_b, 0, 2)
        atm_chunk(buf_b, buf_a, 1, 0, False)
        for copy in edge_copies():
            copy.wait_recv()
        top[0, TAB - 1 : TAB] = qrow[0, 7:8]
        top[0, TAB + CX : TAB + CX + 1] = qrow[1, 0:1]
        for g in range(8):
            ends = jnp.where(lane == 0, pltpu.roll(qcol[0], (128 - g) % 128, 1), pltpu.roll(qcol[1], 126 - g, 1))
            atm_batch(top, top2, 0, 1, ends[None], g)
        cool(top, top2)
        heat = c2 * (top2[0, TAB : TAB + CX] - forc[3])
        out_flux[0, 0] = heat
        out_flux[0, 1] = forc[2] - 0.5 * heat
        out_flux[0, 2] = speed * forc[0]
        out_flux[0, 3] = speed * forc[1]

    @pl.when(is_ocn)
    def _():
        out_flux[0, 0] = speed * forc[0]
        out_flux[0, 1] = speed * forc[1]

    for c in range(2):
        high, low = hi_lo(out_flux[0, c])
        fb[CX * c : CX * (c + 1)] = high
        fb[2 * CX + CX * c : 2 * CX + CX * (c + 1)] = low
    one, none = jnp.array(1, BF16), jnp.array(0, BF16)

    def pick(t, carry):
        n = lax.rem(t + 5, 9)
        at = pl.multiple_of(n * CAP, CAP)
        source = remap[0:1, pl.ds(at, CAP)]
        weight = remap[4:5, pl.ds(at, CAP)].astype(F32)
        col = (source & (CY - 1)).astype(F32).astype(BF16)
        hot = jnp.where(wide(iota[...], CAP // 128) == col, one, none)
        product = jnp.dot(fb[...], hot, preferred_element_type=F32)
        here = lax.broadcasted_iota(jnp.int32, (CX, CAP), 0) == (source >> 8)
        for c in range(2):
            both = product[CX * c : CX * (c + 1)] + product[2 * CX + CX * c : 2 * CX + CX * (c + 1)]
            val_s[n, c : c + 1] = jnp.sum(jnp.where(here, both, 0.0), 0, keepdims=True) * weight

        @pl.when(n != 4)
        def _():
            val_copy(n).start()

        @pl.when(jnp.logical_and(is_ocn, n != 4))
        def _():
            lnk_copy(n).start()

        return carry

    lax.fori_loop(0, 9, pick, 0)
    lnk_r[4] = lnk_s[4]
    val_r[4] = val_s[4]
    acc[...] = jnp.zeros_like(acc)

    def add(t, arrived, fields):
        n = lax.rem(t + 4, 9)
        pl.when(n != 4)(lambda: arrived(n))
        target = lnk_r[n, 0:1]
        weight = lnk_r[n, 1:2].astype(F32).astype(BF16)
        col = (target & (CY - 1)).astype(F32).astype(BF16)
        row = (target >> 8).astype(F32).astype(BF16)
        index = wide(iota[...], CAP // 128)
        hot = jnp.where(index == col, one, none)
        here = index[:CX] == row
        high0, low0 = hi_lo(val_r[n, 0:1])
        high1, low1 = hi_lo(val_r[n, 1:2])
        spread = jnp.concatenate(
            [jnp.where(here, x, none) for x in (high0, high1, low0, low1, weight)[:fields]], 0
        )
        acc[0 : fields * CX] += lax.dot_general(
            spread, hot, (((1,), (1,)), ((), ())), preferred_element_type=F32
        )

    per_copy = pltpu.make_async_remote_copy(
        per.at[0], per.at[1], ps_sem, pr_sem, device_id=(1 - sec, tx, ty), device_id_type=MESH
    )

    @pl.when(is_atm)
    def _():
        def arrived(n):
            lnk_pass(n).wait_recv()
            val_copy(n).wait_recv()

        def step(t, carry):
            add(t, arrived, 4)
            return carry

        lax.fori_loop(0, 9, step, 0)
        per_copy.wait_recv()

    @pl.when(is_ocn)
    def _():
        first_halos()
        halo_send(0, 0)
        other_halos()
        for n in range(9):
            if n != 4:
                lnk_copy(n).wait_recv()
                lnk_pass(n).start()

        def step(t, carry):
            add(t, lambda n: val_copy(n).wait_recv(), 5)
            return carry

        lax.fori_loop(0, 9, step, 0)
        per[0] = 1.0 / jnp.maximum(acc[4 * CX : 5 * CX], 1.0)
        per_copy.start()
        per[1] = per[0]

    rem[0:CX] = (acc[0:CX] + acc[2 * CX : 3 * CX]) * per[1]
    rem[CX : 2 * CX] = (acc[CX : 2 * CX] + acc[3 * CX : 4 * CX]) * per[1]

    hand_over = pltpu.make_async_remote_copy(
        rem, hst, rs_sem, rr_sem, device_id=(1 - sec, tx, ty), device_id_type=MESH
    )

    def along_ty(d):
        return pltpu.make_async_remote_copy(
            red, red1.at[d], p1s_sem.at[d], p1r_sem.at[d],
            device_id=near(0, d), device_id_type=MESH,
        )

    def along_tx(d):
        return pltpu.make_async_remote_copy(
            red1.at[0], red2.at[d], p2s_sem.at[d], p2r_sem.at[d],
            device_id=near(d, 0), device_id_type=MESH,
        )

    def folded(plane):
        total = plane[0:8]
        for g in range(1, 8):
            total = total + plane[8 * g : 8 * g + 8]
        return total

    @pl.when(is_atm)
    def _():
        rem[2 * CX : 2 * CX + 8] = folded(out_flux[0, 0])
        hand_over.start()

        def second(ch, carry):
            atm_chunk(buf_b, buf_a, 1, ch)
            return carry

        lax.fori_loop(1, NCH, second, 0)

        def third(ch, carry):
            atm_chunk(buf_a, out_state, 2, ch)
            return carry

        lax.fori_loop(0, NCH, third, 0)
        hand_over.wait_send()
        for s in range(3):
            for ch in range(NCH):
                for copy in halo_copies(s, ch):
                    copy.wait_send()

    @pl.when(is_ocn)
    def _():
        out_flux[0, 2] = surface * rem[0:CX]
        out_flux[0, 3] = surface * rem[CX : 2 * CX]
        level8 = lax.broadcasted_iota(jnp.int32, (LEV, 8, 128), 0).astype(F32)
        dec[...] = 0.5 * jnp.exp(level8 * (-1 / 8))
        halo_wait(0, 0)
        coefficients()

        out_state[0, OLEV:LEV] = buf_a[OLEV:LEV, TAB : TAB + CX]

        def ocn_batch(src, dst, k, count, ends, g):
            part, at = slice(8 * g, 8 * g + 8), TAB + 8 * g
            c_up, c_down, c_left, c_right, c_mix, c_own = [cf[i, part][None] for i in range(6)]
            d_up, d_down, d_left, d_right = [cf[i, part][None] for i in range(6, 10)]
            own = lev[part].astype(F32)[None]
            sx, sy = out_flux[0, 2, part][None], out_flux[0, 3, part][None]
            here = jnp.concatenate(
                [jnp.full((1, 8, CY), jnp.asarray(k + i, jnp.int32).astype(F32), F32) for i in range(count)], 0
            )
            fade = dec[pl.ds(k, count)]
            value = src[pl.ds(k, count), at : at + 8]
            before = src[pl.ds(jnp.maximum(k - 1, 0), 1), at : at + 8]
            after = src[pl.ds(k + count, 1), at : at + 8]
            before = jnp.concatenate([before, value[:-1]], 0)
            after = jnp.concatenate([value[1:], after], 0)
            up = src[pl.ds(k, count), at - 1 : at + 7]
            down = src[pl.ds(k, count), at + 1 : at + 9]
            left, right = sides(value, ends)
            new = c_own * value + c_mix * (jnp.where(here + 1.0 < own, after, value) + before)
            new = new + (
                c_up * jnp.where(here < d_up, up, value) + c_down * jnp.where(here < d_down, down, value)
            )
            new = new + (
                c_left * jnp.where(here < d_left, left, value)
                + c_right * jnp.where(here < d_right, right, value)
            )
            new = new - jnp.concatenate([fade, fade], 2) * (sx * (down - up) + sy * (right - left))
            put(dst, k, count, g, jnp.where(here < own, new, value))

        def ocn_chunk(src, dst, s, ch):
            unpack_edges(src, s, ch)

            def batch(b, carry):
                for g in range(8):
                    ends = ends_of(g, b * STACK, STACK)
                    ocn_batch(src, dst, ch * CH + b * STACK, STACK, ends, g)
                return carry

            batches = jnp.minimum(CH, OLEV - ch * CH) // STACK
            lax.fori_loop(0, batches, batch, 0)

        def first(ch, carry):
            @pl.when(ch > 0)
            def _():
                halo_wait(0, ch)

            ocn_chunk(buf_a, buf_b, 0, ch)
            pack_edges(buf_b, 1, ch)
            halo_send(1, ch)
            return carry

        lax.fori_loop(0, NCH, first, 0)

        def second(ch):
            halo_wait(1, ch)
            ocn_chunk(buf_b, out_state, 1, ch)

        second(0)

        gain = surface * 4.0 * c2
        hand_over.wait_recv()
        heat_in, fresh_in = hst[0:CX], hst[CX : 2 * CX]
        for i, plane in enumerate((hst[2 * CX : 2 * CX + 8] - folded(surface * heat_in), folded(surface))):
            red[8 * i : 8 * i + 8] = plane[:, :128] + plane[:, 128:]
        for d in range(1, 8):
            along_ty(d).start()
        qb[...] = buf_b[0, TAB : TAB + CX] + gain * (heat_in + 0.3 * fresh_in)
        edge_send()
        second(1)
        total = red[...]
        for d in range(1, 8):
            along_ty(d).wait_recv()
            total = total + red1[d]
        red1[0] = total
        for d in range(1, 8):
            along_tx(d).start()
        second(2)
        for d in range(1, 8):
            along_tx(d).wait_recv()
            total = total + red2[d]
        fix = jnp.sum(total[0:8], keepdims=True) / jnp.maximum(jnp.sum(total[8:16], keepdims=True), 1.0)
        flux0 = surface * (heat_in + fix)
        flux1 = surface * fresh_in
        out_flux[0, 0] = flux0
        out_flux[0, 1] = flux1
        buf_b[0, TAB : TAB + CX] = qb[...] + gain * fix
        for copy in edge_copies():
            copy.wait_recv()

        def gain_of(c2_edge, depth_edge):
            return (depth_edge > 0.0).astype(F32) * 4.0 * c2_edge

        for side, at, inner in ((0, TAB - 1, 7), (1, TAB + CX, 0)):
            edge = rrecv[0, 0, side]
            buf_b[0, at : at + 1] = qrow[side, inner : inner + 1] + fix * gain_of(
                edge[CH + 2 : CH + 3], edge[CH + 1 : CH + 2]
            )
        unpack_columns(1, 0)
        for g in range(8):
            base, part = lanes_of(g)
            low, high = crecv[0, 0, 0, part], crecv[0, 0, 1, part]
            at_depth, at_c2 = base + CH + 1, base + CH + 2
            low = gain_of(pltpu.roll(low, 128 - at_c2, 1), pltpu.roll(low, 128 - at_depth, 1))
            high = gain_of(pltpu.roll(high, 126 - at_c2, 1), pltpu.roll(high, 126 - at_depth, 1))
            ends = jnp.where(
                lane == 0,
                pltpu.roll(qcol[0], (128 - g) % 128, 1) + fix * low,
                pltpu.roll(qcol[1], 126 - g, 1) + fix * high,
            )
            ends = jnp.concatenate([ends[None], ends_of(g, 1, 1)], 0)
            ocn_batch(buf_b, out_state, 0, 2, ends, g)
        out_state[0, 0] = out_state[0, 0] + gain * (flux0 + 0.3 * flux1)
        for s in range(2):
            for ch in range(NCH):
                for copy in halo_copies(s, ch):
                    copy.wait_send()
        for d in range(1, 8):
            along_ty(d).wait_send()
            along_tx(d).wait_send()
        per_copy.wait_send()
        for n in range(9):
            if n != 4:
                lnk_copy(n).wait_send()
                lnk_pass(n).wait_send()

    for copy in edge_copies():
        copy.wait_send()
    for n in range(9):
        if n != 4:
            val_copy(n).wait_send()


def write_out(mid, flux, out_state, out_flux, sem):
    copies = [
        pltpu.make_async_copy(mid.at[:, pl.ds(12 * i, 12)], out_state.at[:, pl.ds(12 * i, 12)], sem.at[i])
        for i in range(6)
    ] + [pltpu.make_async_copy(flux, out_flux, sem.at[6])]
    for copy in copies:
        copy.start()
    for copy in copies:
        copy.wait()


def on_device(state, coeffs, forcing, levels, remap):
    vmem = pl.BlockSpec(memory_space=pltpu.VMEM)
    anywhere = pl.BlockSpec(memory_space=pl.ANY)
    hbm = pl.BlockSpec(memory_space=pltpu.HBM)
    dma = pltpu.SemaphoreType.DMA
    mid, flux = pl.pallas_call(
        kernel,
        out_shape=(
            pltpu.VMEM((1, LEV, CX, CY), F32),
            pltpu.VMEM((1, 4, CX, CY), F32),
        ),
        in_specs=[hbm] * 5,
        out_specs=(vmem, vmem),
        scratch_shapes=[
            pltpu.VMEM((1, 3, CX, CY), F32),
            pltpu.VMEM((4, CX, CY), F32),
            pltpu.VMEM((CX, CY), jnp.int32),
            pltpu.VMEM((5, 9 * CAP), jnp.int32),
            pltpu.VMEM((LEV, CX + 16, CY), F32),
            pltpu.VMEM((LEV, CX + 16, CY), F32),
            pltpu.VMEM((2, CX + 16, CY), F32),
            pltpu.VMEM((2, CX + 16, CY), F32),
            pltpu.VMEM((3, NCH, 2, 32, CY), F32),
            pltpu.VMEM((3, NCH, 2, 16, 128), F32),
            pltpu.VMEM((3, NCH, 2, 32, CY), F32),
            pltpu.VMEM((3, NCH, 2, 16, 128), F32),
            pltpu.VMEM((2, 16, 128), F32),
            pltpu.VMEM((10, CX, CY), F32),
            pltpu.VMEM((9, 2, CAP), jnp.int32),
            pltpu.VMEM((9, 2, CAP), jnp.int32),
            pltpu.VMEM((9, 2, CAP), F32),
            pltpu.VMEM((9, 2, CAP), F32),
            pltpu.VMEM((5 * CX, CY), F32),
            pltpu.VMEM((4 * CX, CY), BF16),
            pltpu.VMEM((CY, 128), BF16),
            pltpu.VMEM((LEV, 8, 128), F32),
            pltpu.VMEM((2 * CX + 8, CY), F32),
            pltpu.VMEM((2 * CX + 8, CY), F32),
            pltpu.VMEM((2, CX, CY), F32),
            pltpu.VMEM((CX, CY), F32),
            pltpu.VMEM((2, 8, 128), F32),
            pltpu.VMEM((2, 8, CY), F32),
            pltpu.VMEM((2, 8, 128), F32),
            pltpu.VMEM((16, 128), F32),
            pltpu.VMEM((8, 16, 128), F32),
            pltpu.VMEM((8, 16, 128), F32),
            dma((NCH + 4,)),
            dma((3, NCH, 4)),
            dma((3, NCH, 4)),
            dma((9,)),
            dma((9,)),
            dma((9,)),
            dma((9,)),
            dma,
            dma,
            dma((9,)),
            dma((9,)),
            dma,
            dma,
            dma((4,)),
            dma((4,)),
            dma((8,)),
            dma((8,)),
            dma((8,)),
            dma((8,)),
        ],
        compiler_params=pltpu.CompilerParams(
            collective_id=0, has_side_effects=True, vmem_limit_bytes=59 << 20
        ),
        name="window",
    )(state, coeffs, forcing, levels, remap)
    return pl.pallas_call(
        write_out,
        out_shape=(
            jax.ShapeDtypeStruct((1, LEV, CX, CY), F32),
            jax.ShapeDtypeStruct((1, 4, CX, CY), F32),
        ),
        in_specs=[vmem, vmem],
        out_specs=(anywhere, anywhere),
        scratch_shapes=[dma((7,))],
        compiler_params=pltpu.CompilerParams(vmem_limit_bytes=4 << 20),
        name="write_out",
    )(mid, flux)


def solution(mesh):
    return jax.shard_map(
        on_device,
        mesh=mesh,
        in_specs=(
            P("sec", None, "tx", "ty"),
            P("sec", None, "tx", "ty"),
            P(None, "tx", "ty"),
            P("tx", "ty"),
            P(None, ("tx", "ty")),
        ),
        out_specs=(P("sec", None, "tx", "ty"), P("sec", None, "tx", "ty")),
        check_vma=False,
    )
```

```python
import jax
import jax.numpy as jnp
from jax import lax
from jax.experimental import pallas as pl
from jax.experimental.pallas import tpu as pltpu
from jax.sharding import PartitionSpec as P

LEV, OLEV, CX, CY = 72, 60, 64, 256
CAP = 4096
TAB = 8
CH = 24
NCH = LEV // CH
STACK = 6
F32, BF16 = jnp.float32, jnp.bfloat16
MESH = pl.DeviceIdType.MESH


def hi_lo(x):
    high = x.astype(BF16)
    return high, (x - high.astype(F32)).astype(BF16)


def wide(x, count):
    return jnp.concatenate([x] * count, 1)


def kernel(
    state, coef_in, forc_in, lev_in, remap_in, out_state, out_flux,
    coef, forc, lev, remap, buf_a, buf_b, top, top2, rsend, csend, rrecv, crecv, ccomb, cf, lnk_s, lnk_r, val_s, val_r, acc, fb, iota,
    dec, rem, hst, per, qb, qcs, qrow, qcol, red, red1, red2,
    in_sem, hs_sem, hr_sem, ls_sem, lr_sem, fs_sem, fr_sem, ps_sem, pr_sem, vs_sem, vr_sem, rs_sem, rr_sem,
    qs_sem, qr_sem, p1s_sem, p1r_sem, p2s_sem, p2r_sem,
):
    sec, tx, ty = lax.axis_index("sec"), lax.axis_index("tx"), lax.axis_index("ty")
    is_atm = sec == 0
    is_ocn = sec == 1

    def near(dx, dy):
        return (sec, lax.rem(tx + dx + 8, 8), lax.rem(ty + dy + 8, 8))

    barrier = pltpu.get_barrier_semaphore()
    for dx in (-1, 0, 1, 4):
        for dy in (-1, 0, 1):
            if dx != 0 or dy != 0:
                pl.semaphore_signal(barrier, 1, device_id=near(dx, dy), device_id_type=MESH)
    for dy in range(2, 7):
        pl.semaphore_signal(barrier, 1, device_id=near(0, dy), device_id_type=MESH)
    for dx in (2, 3, 5, 6):
        pl.semaphore_signal(barrier, 1, device_id=near(dx, 0), device_id_type=MESH)
    pl.semaphore_signal(barrier, 1, device_id=(1 - sec, tx, ty), device_id_type=MESH)

    def state_in(ch):
        return pltpu.make_async_copy(
            state.at[0, pl.ds(ch * CH, CH)],
            buf_a.at[pl.ds(ch * CH, CH), pl.ds(TAB, CX)],
            in_sem.at[ch],
        )

    small_in = [
        pltpu.make_async_copy(source, there, in_sem.at[NCH + i])
        for i, (source, there) in enumerate(
            ((coef_in, coef), (lev_in, lev), (forc_in, forc), (remap_in, remap))
        )
    ]
    for copy in small_in[:3]:
        copy.start()
    state_in(0).start()
    small_in[3].start()
    for ch in range(1, NCH):
        state_in(ch).start()
    iota[...] = lax.broadcasted_iota(jnp.int32, (CY, 128), 0).astype(F32).astype(BF16)
    for copy in small_in[:3]:
        copy.wait()

    kap, mix, c2 = coef[0, 0], coef[0, 1], coef[0, 2]
    depth = jnp.where(is_atm, jnp.full((CX, CY), float(LEV), F32), lev[...].astype(F32))
    surface = (lev[...] > 0).astype(F32)

    def target_of(n):
        row_step = n // 3
        return near(row_step - 1 + 3 * (row_step // 2), n % 3 - 1)

    def lnk_copy(n):
        return pltpu.make_async_remote_copy(
            lnk_s.at[n], lnk_r.at[n], ls_sem.at[n], lr_sem.at[n],
            device_id=target_of(n), device_id_type=MESH,
        )

    def lnk_pass(n):
        return pltpu.make_async_remote_copy(
            lnk_r.at[n], lnk_r.at[n], fs_sem.at[n], fr_sem.at[n],
            device_id=(1 - sec, tx, ty), device_id_type=MESH,
        )

    def val_copy(n):
        return pltpu.make_async_remote_copy(
            val_s.at[n], val_r.at[n], vs_sem.at[n], vr_sem.at[n],
            device_id=target_of(n), device_id_type=MESH,
        )

    def halo_copies(s, ch):
        out = []
        for d, (there, low) in enumerate(
            ((near(1, 0), 0), (near(-1, 0), 1), (near(0, 1), 0), (near(0, -1), 1))
        ):
            if d < 2:
                count = CH + 8 if isinstance(ch, int) and (s, ch) == (0, 0) else CH
                source = rsend.at[s, ch, low, pl.ds(0, count)]
                recv = rrecv.at[s, ch, low, pl.ds(0, count)]
            else:
                source, recv = csend.at[s, ch, low], crecv.at[s, ch, low]
            out.append(
                pltpu.make_async_remote_copy(
                    source, recv, hs_sem.at[s, ch, d], hr_sem.at[s, ch, d],
                    device_id=there, device_id_type=MESH,
                )
            )
        return out

    def edge_copies():
        moves = (
            (qb.at[CX - 8 : CX], qrow.at[0], near(1, 0)),
            (qb.at[0:8], qrow.at[1], near(-1, 0)),
            (qcs.at[0], qcol.at[0], near(0, 1)),
            (qcs.at[1], qcol.at[1], near(0, -1)),
        )
        return [
            pltpu.make_async_remote_copy(
                source, there, qs_sem.at[i], qr_sem.at[i], device_id=device, device_id_type=MESH
            )
            for i, (source, there, device) in enumerate(moves)
        ]

    lane = lax.broadcasted_iota(jnp.int32, (8, 128), 1)
    lane3 = lax.broadcasted_iota(jnp.int32, (1, 8, 128), 2)

    def lanes_of(g):
        return 32 * (g % 4), slice(8 * (g // 4), 8 * (g // 4) + 8)

    def pack_pair(both, at, packed):
        ends = pltpu.roll(jnp.where(lane < 64, both[:, :128], both[:, 128:]), at + 1, 1)
        return jnp.where(lane == at, ends, packed[0]), jnp.where(lane == at + 1, ends, packed[1])

    def pack_edges(src, s, ch, extras=()):
        for q in range(2):
            packed = jnp.zeros((8, 128), F32), jnp.zeros((8, 128), F32)
            for g in range(4 * q, 4 * q + 4):
                base, part = lanes_of(g)
                for i in range(CH + len(extras)):
                    if i < CH:
                        both = src[ch * CH + i, TAB + 8 * g : TAB + 8 * g + 8]
                    else:
                        both = extras[i - CH][8 * g : 8 * g + 8]
                    packed = pack_pair(both, base + i, packed)
            csend[s, ch, 0, part] = packed[0]
            csend[s, ch, 1, part] = packed[1]
        for i in range(0, CH, 8):
            rsend[s, ch, 0, i : i + 8] = src[pl.ds(ch * CH + i, 8), TAB + CX - 1]
            rsend[s, ch, 1, i : i + 8] = src[pl.ds(ch * CH + i, 8), TAB]

    def halo_send(s, ch):
        for copy in halo_copies(s, ch):
            copy.start()

    def edge_send():
        packed = jnp.zeros((8, 128), F32), jnp.zeros((8, 128), F32)
        for g in range(8):
            packed = pack_pair(qb[8 * g : 8 * g + 8], g, packed)
        qcs[0], qcs[1] = packed
        for copy in edge_copies():
            copy.start()

    def unpack_columns(s, ch):
        ccomb[0] = crecv[s, ch, 0]
        ccomb[1] = pltpu.roll(crecv[s, ch, 1], 126, 1)

    def unpack_edges(src, s, ch):
        unpack_columns(s, ch)
        src[pl.ds(ch * CH, CH), TAB - 1] = rrecv[s, ch, 0, 0:CH]
        src[pl.ds(ch * CH, CH), TAB + CX] = rrecv[s, ch, 1, 0:CH]

    def halo_wait(s, ch):
        for copy in halo_copies(s, ch):
            copy.wait_recv()

    def sides(value, ends):
        first, last = value[:, :, :128], value[:, :, 128:]
        right_a, right_b = pltpu.roll(first, 1, 2), pltpu.roll(last, 1, 2)
        left_a, left_b = pltpu.roll(first, 127, 2), pltpu.roll(last, 127, 2)
        left = jnp.concatenate(
            [jnp.where(lane3 == 0, ends, right_a), jnp.where(lane3 == 0, right_a, right_b)], 2
        )
        right = jnp.concatenate(
            [jnp.where(lane3 == 127, left_b, left_a), jnp.where(lane3 == 127, ends, left_b)], 2
        )
        return left, right

    def ends_of(g, i, count):
        base, part = lanes_of(g)
        low, high = ccomb[0, part], ccomb[1, part]
        out = []
        for j in range(count):
            at = base + i + j
            out.append(pltpu.roll(jnp.where(lane == at, low, high), lax.rem(128 - at, 128), 1)[None])
        return jnp.concatenate(out, 0)

    def put(dst, k, count, g, value):
        if dst is out_state:
            out_state[0, pl.ds(k, count), 8 * g : 8 * g + 8] = value
        else:
            dst[pl.ds(k, count), TAB + 8 * g : TAB + 8 * g + 8] = value

    def atm_batch(src, dst, k, count, ends, g):
        part, at = slice(8 * g, 8 * g + 8), TAB + 8 * g
        c_up, c_down, c_left, c_right, c_mix, c_own = [cf[i, part][None] for i in range(6)]
        value = src[pl.ds(k, count), at : at + 8]
        before = src[pl.ds(jnp.maximum(k - 1, 0), 1), at : at + 8]
        after = src[pl.ds(jnp.minimum(k + count, LEV - 1), 1), at : at + 8]
        if count > 1:
            before = jnp.concatenate([before, value[:-1]], 0)
            after = jnp.concatenate([value[1:], after], 0)
        up = src[pl.ds(k, count), at - 1 : at + 7]
        down = src[pl.ds(k, count), at + 1 : at + 9]
        left, right = sides(value, ends)
        new = c_own * value + c_mix * (before + after)
        new = new + (c_up * up + c_down * down) + (c_left * left + c_right * right)
        put(dst, k, count, g, new)

    def cool(src, dst):
        rows = slice(TAB, TAB + CX)
        heat = coef[0, 2] * (src[0, rows] - forc[3])
        if dst is out_state:
            dst[0, 0] = dst[0, 0] - heat
        else:
            dst[0, rows] = dst[0, rows] - heat

    def atm_chunk(src, dst, s, ch, wait=True, STACK=12):
        if wait:
            halo_wait(s, ch)
        unpack_edges(src, s, ch)

        def batch(b, carry):
            for g in range(8):
                ends = ends_of(g, b * STACK, STACK)
                atm_batch(src, dst, ch * CH + b * STACK, STACK, ends, g)
            return carry

        lax.fori_loop(0, CH // STACK, batch, 0)
        if isinstance(ch, int):
            if ch == 0:
                cool(src, dst)
        else:
            pl.when(ch == 0)(lambda: cool(src, dst))
        if s < 2:
            pack_edges(dst, s + 1, ch)
            halo_send(s + 1, ch)

    lane_all = lax.broadcasted_iota(jnp.int32, (CX, CY), 1)

    def around(plane, at):
        low_row = rrecv[0, 0, 0, CH + at : CH + at + 1]
        high_row = rrecv[0, 0, 1, CH + at : CH + at + 1]
        low_col, high_col = [], []
        for g in range(8):
            base, part = lanes_of(g)
            low_col.append(crecv[0, 0, 0, part][:, base + CH + at : base + CH + at + 1])
            high_col.append(crecv[0, 0, 1, part][:, base + CH + at + 1 : base + CH + at + 2])
        low_col, high_col = jnp.concatenate(low_col, 0), jnp.concatenate(high_col, 0)
        return (
            jnp.concatenate([low_row, plane[:-1]], 0),
            jnp.concatenate([plane[1:], high_row], 0),
            jnp.where(lane_all == 0, low_col, pltpu.roll(plane, 1, 1)),
            jnp.where(lane_all == CY - 1, high_col, pltpu.roll(plane, CY - 1, 1)),
        )

    def coefficients():
        total = jnp.zeros((CX, CY), F32)
        for at, other in enumerate(around(kap, 0)):
            half = 0.5 * (kap + other)
            cf[at] = half
            total = total + half
        cf[4] = mix
        cf[5] = (1.0 - total) - 2.0 * mix
        for at, other in enumerate(around(depth, 1)):
            cf[6 + at] = other

    def first_halos():
        for side, row in ((0, CX - 1), (1, 0)):
            rsend[0, 0, side, CH : CH + 8] = jnp.zeros((8, CY), F32)
            for at, plane in enumerate((kap, depth, c2)):
                rsend[0, 0, side, CH + at : CH + at + 1] = plane[row : row + 1]
        state_in(0).wait()
        pack_edges(buf_a, 0, 0, (kap, depth, c2))

    def other_halos():
        def more(ch, carry):
            state_in(ch).wait()
            pack_edges(buf_a, 0, ch)
            halo_send(0, ch)
            return carry

        lax.fori_loop(1, NCH, more, 0)

    pl.when(is_atm)(first_halos)

    def stage_links():
        small_in[3].wait()
        for n in range(9):
            lnk_s[n] = remap[3:5, n * CAP : (n + 1) * CAP]

    pl.when(is_ocn)(stage_links)
    pl.semaphore_wait(barrier, 21)

    speed = 0.2 * jnp.sqrt(1.0 + forc[0] * forc[0] + forc[1] * forc[1])

    @pl.when(is_atm)
    def _():
        halo_send(0, 0)
        other_halos()
        stage_links()
        halo_wait(0, 0)
        coefficients()
        atm_chunk(buf_a, buf_b, 0, 0, False)
        atm_chunk(buf_a, buf_b, 0, 1)
        halo_wait(1, 0)
        unpack_edges(buf_b, 1, 0)
        for g in range(8):
            atm_batch(buf_b, top, 0, 2, ends_of(g, 0, 2), g)
        cool(buf_b, top)
        qb[...] = top[0, TAB : TAB + CX]
        edge_send()
        atm_chunk(buf_a, buf_b, 0, 2)
        atm_chunk(buf_b, buf_a, 1, 0, False)
        for copy in edge_copies():
            copy.wait_recv()
        top[0, TAB - 1 : TAB] = qrow[0, 7:8]
        top[0, TAB + CX : TAB + CX + 1] = qrow[1, 0:1]
        for g in range(8):
            ends = jnp.where(lane == 0, pltpu.roll(qcol[0], (128 - g) % 128, 1), pltpu.roll(qcol[1], 126 - g, 1))
            atm_batch(top, top2, 0, 1, ends[None], g)
        cool(top, top2)
        heat = c2 * (top2[0, TAB : TAB + CX] - forc[3])
        out_flux[0, 0] = heat
        out_flux[0, 1] = forc[2] - 0.5 * heat
        out_flux[0, 2] = speed * forc[0]
        out_flux[0, 3] = speed * forc[1]

    @pl.when(is_ocn)
    def _():
        out_flux[0, 0] = speed * forc[0]
        out_flux[0, 1] = speed * forc[1]

    for c in range(2):
        high, low = hi_lo(out_flux[0, c])
        fb[CX * c : CX * (c + 1)] = high
        fb[2 * CX + CX * c : 2 * CX + CX * (c + 1)] = low
    one, none = jnp.array(1, BF16), jnp.array(0, BF16)

    def pick(t, carry):
        m = lax.rem(t + 2, 3)
        at = pl.multiple_of(m * 3 * CAP, 3 * CAP)
        source = remap[0:1, pl.ds(at, 3 * CAP)]
        weight = remap[4:5, pl.ds(at, 3 * CAP)].astype(F32)
        col = (source & (CY - 1)).astype(F32).astype(BF16)
        hot = jnp.where(wide(iota[...], 3 * CAP // 128) == col, one, none)
        product = jnp.dot(fb[...], hot, preferred_element_type=F32)
        here = lax.broadcasted_iota(jnp.int32, (CX, 3 * CAP), 0) == (source >> 8)
        for c in range(2):
            both = product[CX * c : CX * (c + 1)] + product[2 * CX + CX * c : 2 * CX + CX * (c + 1)]
            picked = jnp.sum(jnp.where(here, both, 0.0), 0, keepdims=True) * weight
            for j in range(3):
                val_s[3 * m + j, c : c + 1] = picked[:, j * CAP : (j + 1) * CAP]
        for j in range(3):
            n = 3 * m + j

            @pl.when(n != 4)
            def _(n=n):
                val_copy(n).start()

            @pl.when(jnp.logical_and(is_ocn, n != 4))
            def _(n=n):
                lnk_copy(n).start()

        return carry

    lax.fori_loop(0, 3, pick, 0)
    lnk_r[4] = lnk_s[4]
    val_r[4] = val_s[4]
    acc[...] = jnp.zeros_like(acc)

    def add(t, arrived, fields):
        m = lax.rem(t + 2, 3)
        for j in range(3):
            pl.when(3 * m + j != 4)(lambda j=j: arrived(3 * m + j))

        def three(ref, row):
            return jnp.concatenate([ref[3 * m + j, row : row + 1] for j in range(3)], 1)

        target = three(lnk_r, 0)
        weight = three(lnk_r, 1).astype(F32).astype(BF16)
        col = (target & (CY - 1)).astype(F32).astype(BF16)
        row = (target >> 8).astype(F32).astype(BF16)
        index = wide(iota[...], 3 * CAP // 128)
        hot = jnp.where(index == col, one, none)
        here = index[:CX] == row
        high0, low0 = hi_lo(three(val_r, 0))
        high1, low1 = hi_lo(three(val_r, 1))
        spread = jnp.concatenate(
            [jnp.where(here, x, none) for x in (high0, high1, low0, low1, weight)[:fields]], 0
        )
        acc[0 : fields * CX] += lax.dot_general(
            spread, hot, (((1,), (1,)), ((), ())), preferred_element_type=F32
        )

    per_copy = pltpu.make_async_remote_copy(
        per.at[0], per.at[1], ps_sem, pr_sem, device_id=(1 - sec, tx, ty), device_id_type=MESH
    )

    @pl.when(is_atm)
    def _():
        def arrived(n):
            lnk_pass(n).wait_recv()
            val_copy(n).wait_recv()

        def step(t, carry):
            add(t, arrived, 4)
            return carry

        lax.fori_loop(0, 3, step, 0)
        per_copy.wait_recv()

    @pl.when(is_ocn)
    def _():
        first_halos()
        halo_send(0, 0)
        other_halos()
        for n in range(9):
            if n != 4:
                lnk_copy(n).wait_recv()
                lnk_pass(n).start()

        def step(t, carry):
            add(t, lambda n: val_copy(n).wait_recv(), 5)
            return carry

        lax.fori_loop(0, 3, step, 0)
        per[0] = 1.0 / jnp.maximum(acc[4 * CX : 5 * CX], 1.0)
        per_copy.start()
        per[1] = per[0]

    rem[0:CX] = (acc[0:CX] + acc[2 * CX : 3 * CX]) * per[1]
    rem[CX : 2 * CX] = (acc[CX : 2 * CX] + acc[3 * CX : 4 * CX]) * per[1]

    hand_over = pltpu.make_async_remote_copy(
        rem, hst, rs_sem, rr_sem, device_id=(1 - sec, tx, ty), device_id_type=MESH
    )

    def along_ty(d):
        return pltpu.make_async_remote_copy(
            red, red1.at[d], p1s_sem.at[d], p1r_sem.at[d],
            device_id=near(0, d), device_id_type=MESH,
        )

    def along_tx(d):
        return pltpu.make_async_remote_copy(
            red1.at[0], red2.at[d], p2s_sem.at[d], p2r_sem.at[d],
            device_id=near(d, 0), device_id_type=MESH,
        )

    def folded(plane):
        total = plane[0:8]
        for g in range(1, 8):
            total = total + plane[8 * g : 8 * g + 8]
        return total

    @pl.when(is_atm)
    def _():
        rem[2 * CX : 2 * CX + 8] = folded(out_flux[0, 0])
        hand_over.start()

        def second(ch, carry):
            atm_chunk(buf_b, buf_a, 1, ch)
            return carry

        lax.fori_loop(1, NCH, second, 0)

        def third(ch, carry):
            atm_chunk(buf_a, out_state, 2, ch)
            return carry

        lax.fori_loop(0, NCH, third, 0)
        hand_over.wait_send()
        for s in range(3):
            for ch in range(NCH):
                for copy in halo_copies(s, ch):
                    copy.wait_send()

    @pl.when(is_ocn)
    def _():
        out_flux[0, 2] = surface * rem[0:CX]
        out_flux[0, 3] = surface * rem[CX : 2 * CX]
        level8 = lax.broadcasted_iota(jnp.int32, (LEV, 8, 128), 0).astype(F32)
        dec[...] = 0.5 * jnp.exp(level8 * (-1 / 8))
        halo_wait(0, 0)
        coefficients()

        out_state[0, OLEV:LEV] = buf_a[OLEV:LEV, TAB : TAB + CX]

        def ocn_batch(src, dst, k, count, ends, g):
            part, at = slice(8 * g, 8 * g + 8), TAB + 8 * g
            c_up, c_down, c_left, c_right, c_mix, c_own = [cf[i, part][None] for i in range(6)]
            d_up, d_down, d_left, d_right = [cf[i, part][None] for i in range(6, 10)]
            own = lev[part].astype(F32)[None]
            sx, sy = out_flux[0, 2, part][None], out_flux[0, 3, part][None]
            here = jnp.concatenate(
                [jnp.full((1, 8, CY), jnp.asarray(k + i, jnp.int32).astype(F32), F32) for i in range(count)], 0
            )
            fade = dec[pl.ds(k, count)]
            value = src[pl.ds(k, count), at : at + 8]
            before = src[pl.ds(jnp.maximum(k - 1, 0), 1), at : at + 8]
            after = src[pl.ds(k + count, 1), at : at + 8]
            before = jnp.concatenate([before, value[:-1]], 0)
            after = jnp.concatenate([value[1:], after], 0)
            up = src[pl.ds(k, count), at - 1 : at + 7]
            down = src[pl.ds(k, count), at + 1 : at + 9]
            left, right = sides(value, ends)
            new = c_own * value + c_mix * (jnp.where(here + 1.0 < own, after, value) + before)
            new = new + (
                c_up * jnp.where(here < d_up, up, value) + c_down * jnp.where(here < d_down, down, value)
            )
            new = new + (
                c_left * jnp.where(here < d_left, left, value)
                + c_right * jnp.where(here < d_right, right, value)
            )
            new = new - jnp.concatenate([fade, fade], 2) * (sx * (down - up) + sy * (right - left))
            put(dst, k, count, g, jnp.where(here < own, new, value))

        def ocn_chunk(src, dst, s, ch):
            unpack_edges(src, s, ch)

            def batch(b, carry):
                for g in range(8):
                    ends = ends_of(g, b * STACK, STACK)
                    ocn_batch(src, dst, ch * CH + b * STACK, STACK, ends, g)
                return carry

            batches = jnp.minimum(CH, OLEV - ch * CH) // STACK
            lax.fori_loop(0, batches, batch, 0)

        def first(ch, carry):
            @pl.when(ch > 0)
            def _():
                halo_wait(0, ch)

            ocn_chunk(buf_a, buf_b, 0, ch)
            pack_edges(buf_b, 1, ch)
            halo_send(1, ch)
            return carry

        lax.fori_loop(0, NCH, first, 0)

        def second(ch):
            halo_wait(1, ch)
            ocn_chunk(buf_b, out_state, 1, ch)

        second(0)

        gain = surface * 4.0 * c2
        hand_over.wait_recv()
        heat_in, fresh_in = hst[0:CX], hst[CX : 2 * CX]
        for i, plane in enumerate((hst[2 * CX : 2 * CX + 8] - folded(surface * heat_in), folded(surface))):
            red[8 * i : 8 * i + 8] = plane[:, :128] + plane[:, 128:]
        for d in range(1, 8):
            along_ty(d).start()
        qb[...] = buf_b[0, TAB : TAB + CX] + gain * (heat_in + 0.3 * fresh_in)
        edge_send()
        second(1)
        total = red[...]
        for d in range(1, 8):
            along_ty(d).wait_recv()
            total = total + red1[d]
        red1[0] = total
        for d in range(1, 8):
            along_tx(d).start()
        second(2)
        for d in range(1, 8):
            along_tx(d).wait_recv()
            total = total + red2[d]
        fix = jnp.sum(total[0:8], keepdims=True) / jnp.maximum(jnp.sum(total[8:16], keepdims=True), 1.0)
        flux0 = surface * (heat_in + fix)
        flux1 = surface * fresh_in
        out_flux[0, 0] = flux0
        out_flux[0, 1] = flux1
        buf_b[0, TAB : TAB + CX] = qb[...] + gain * fix
        for copy in edge_copies():
            copy.wait_recv()

        def gain_of(c2_edge, depth_edge):
            return (depth_edge > 0.0).astype(F32) * 4.0 * c2_edge

        for side, at, inner in ((0, TAB - 1, 7), (1, TAB + CX, 0)):
            edge = rrecv[0, 0, side]
            buf_b[0, at : at + 1] = qrow[side, inner : inner + 1] + fix * gain_of(
                edge[CH + 2 : CH + 3], edge[CH + 1 : CH + 2]
            )
        unpack_columns(1, 0)
        for g in range(8):
            base, part = lanes_of(g)
            low, high = crecv[0, 0, 0, part], crecv[0, 0, 1, part]
            at_depth, at_c2 = base + CH + 1, base + CH + 2
            low = gain_of(pltpu.roll(low, 128 - at_c2, 1), pltpu.roll(low, 128 - at_depth, 1))
            high = gain_of(pltpu.roll(high, 126 - at_c2, 1), pltpu.roll(high, 126 - at_depth, 1))
            ends = jnp.where(
                lane == 0,
                pltpu.roll(qcol[0], (128 - g) % 128, 1) + fix * low,
                pltpu.roll(qcol[1], 126 - g, 1) + fix * high,
            )
            ends = jnp.concatenate([ends[None], ends_of(g, 1, 1)], 0)
            ocn_batch(buf_b, out_state, 0, 2, ends, g)
        out_state[0, 0] = out_state[0, 0] + gain * (flux0 + 0.3 * flux1)
        for s in range(2):
            for ch in range(NCH):
                for copy in halo_copies(s, ch):
                    copy.wait_send()
        for d in range(1, 8):
            along_ty(d).wait_send()
            along_tx(d).wait_send()
        per_copy.wait_send()
        for n in range(9):
            if n != 4:
                lnk_copy(n).wait_send()
                lnk_pass(n).wait_send()

    for copy in edge_copies():
        copy.wait_send()
    for n in range(9):
        if n != 4:
            val_copy(n).wait_send()


def write_out(mid, flux, out_state, out_flux, sem):
    copies = [
        pltpu.make_async_copy(mid.at[:, pl.ds(12 * i, 12)], out_state.at[:, pl.ds(12 * i, 12)], sem.at[i])
        for i in range(6)
    ] + [pltpu.make_async_copy(flux, out_flux, sem.at[6])]
    for copy in copies:
        copy.start()
    for copy in copies:
        copy.wait()


def on_device(state, coeffs, forcing, levels, remap):
    vmem = pl.BlockSpec(memory_space=pltpu.VMEM)
    anywhere = pl.BlockSpec(memory_space=pl.ANY)
    hbm = pl.BlockSpec(memory_space=pltpu.HBM)
    dma = pltpu.SemaphoreType.DMA
    mid, flux = pl.pallas_call(
        kernel,
        out_shape=(
            pltpu.VMEM((1, LEV, CX, CY), F32),
            pltpu.VMEM((1, 4, CX, CY), F32),
        ),
        in_specs=[hbm] * 5,
        out_specs=(vmem, vmem),
        scratch_shapes=[
            pltpu.VMEM((1, 3, CX, CY), F32),
            pltpu.VMEM((4, CX, CY), F32),
            pltpu.VMEM((CX, CY), jnp.int32),
            pltpu.VMEM((5, 9 * CAP), jnp.int32),
            pltpu.VMEM((LEV, CX + 16, CY), F32),
            pltpu.VMEM((LEV, CX + 16, CY), F32),
            pltpu.VMEM((2, CX + 16, CY), F32),
            pltpu.VMEM((2, CX + 16, CY), F32),
            pltpu.VMEM((3, NCH, 2, 32, CY), F32),
            pltpu.VMEM((3, NCH, 2, 16, 128), F32),
            pltpu.VMEM((3, NCH, 2, 32, CY), F32),
            pltpu.VMEM((3, NCH, 2, 16, 128), F32),
            pltpu.VMEM((2, 16, 128), F32),
            pltpu.VMEM((10, CX, CY), F32),
            pltpu.VMEM((9, 2, CAP), jnp.int32),
            pltpu.VMEM((9, 2, CAP), jnp.int32),
            pltpu.VMEM((9, 2, CAP), F32),
            pltpu.VMEM((9, 2, CAP), F32),
            pltpu.VMEM((5 * CX, CY), F32),
            pltpu.VMEM((4 * CX, CY), BF16),
            pltpu.VMEM((CY, 128), BF16),
            pltpu.VMEM((LEV, 8, 128), F32),
            pltpu.VMEM((2 * CX + 8, CY), F32),
            pltpu.VMEM((2 * CX + 8, CY), F32),
            pltpu.VMEM((2, CX, CY), F32),
            pltpu.VMEM((CX, CY), F32),
            pltpu.VMEM((2, 8, 128), F32),
            pltpu.VMEM((2, 8, CY), F32),
            pltpu.VMEM((2, 8, 128), F32),
            pltpu.VMEM((16, 128), F32),
            pltpu.VMEM((8, 16, 128), F32),
            pltpu.VMEM((8, 16, 128), F32),
            dma((NCH + 4,)),
            dma((3, NCH, 4)),
            dma((3, NCH, 4)),
            dma((9,)),
            dma((9,)),
            dma((9,)),
            dma((9,)),
            dma,
            dma,
            dma((9,)),
            dma((9,)),
            dma,
            dma,
            dma((4,)),
            dma((4,)),
            dma((8,)),
            dma((8,)),
            dma((8,)),
            dma((8,)),
        ],
        compiler_params=pltpu.CompilerParams(
            collective_id=0, has_side_effects=True, vmem_limit_bytes=59 << 20
        ),
        name="window",
    )(state, coeffs, forcing, levels, remap)
    return pl.pallas_call(
        write_out,
        out_shape=(
            jax.ShapeDtypeStruct((1, LEV, CX, CY), F32),
            jax.ShapeDtypeStruct((1, 4, CX, CY), F32),
        ),
        in_specs=[vmem, vmem],
        out_specs=(anywhere, anywhere),
        scratch_shapes=[dma((7,))],
        compiler_params=pltpu.CompilerParams(vmem_limit_bytes=4 << 20),
        name="write_out",
    )(mid, flux)


def solution(mesh):
    return jax.shard_map(
        on_device,
        mesh=mesh,
        in_specs=(
            P("sec", None, "tx", "ty"),
            P("sec", None, "tx", "ty"),
            P(None, "tx", "ty"),
            P("tx", "ty"),
            P(None, ("tx", "ty")),
        ),
        out_specs=(P("sec", None, "tx", "ty"), P("sec", None, "tx", "ty")),
        check_vma=False,
    )
```
